32 devices in a mesh: ctx: 8 (over z, x), ch: 4 (over y, core).
Axes of the slice: x: 2, y: 2, z: 4, core: 2. Of those that a mesh axis runs over, the one named last changes fastest.
Arguments:
- inputs: float32 [4, 2048, 1024], P(None, 'ctx', 'ch'), may hold values from -6 to 6
- cotangent: float32 [4, 2048, 1024], P(None, 'ctx', 'ch'), may hold values from -6 to 6
- filters: float32 [2048, 1024], P('ctx', 'ch'), may hold values from -6 to 6
Outputs:
- input_grad: float32 [4, 2048, 1024], P(None, 'ctx', 'ch')
- filter_grad: float32 [2048, 1024], P('ctx', 'ch')
The draws below stay inside these ranges and needn't reach their ends.
All inputs are finite; a program needn't handle non-finite values.
Results may differ from the reference program's by a relative error of at most 0.0001.
Values sent between devices are 32-bit elements; how exact they have to be, the bound alone decides.
A program may use at most 128 MiB of HBM per device.

```python
import math
import jax
import jax.numpy as jnp

C = 1024
SEQS = 4
SEQ_LEN = 2048


def block_scale(key, dims, shards, low, largest):
    def one(position, parts):
        steps = jax.random.uniform(jax.random.fold_in(jax.random.fold_in(key, 6), position), (parts,), jnp.float32, low / len(shards), largest / len(shards))
        return jnp.repeat(jnp.exp(steps), dims[position] // parts).reshape((-1,) + (1,) * (len(dims) - position - 1))

    loudness = one(*shards[0])
    for cut in shards[1:]:
        loudness = loudness * one(*cut)
    return loudness


def centred(stream_key, shape, spread, reach, shards=(), kind=jnp.bfloat16):
    drawn = spread * jax.random.normal(stream_key, shape, jnp.float32)
    if shards:
        drawn = drawn * block_scale(stream_key, shape, shards, -0.22, 0.18)
    return jnp.clip(drawn, -reach, reach).astype(kind)


def setup_inputs(seed: int = 0) -> dict:
    seeds = jax.random.split(jax.random.key(seed), 4)
    inputs = centred(seeds[0], (SEQS, SEQ_LEN, C), 1.0, 6.0, ((1, 8), (2, 4)), jnp.float32)
    cotangent = centred(seeds[1], (SEQS, SEQ_LEN, C), 1.0, 6.0, ((1, 8), (2, 4)), jnp.float32)
    filters = centred(seeds[2], (SEQ_LEN, C), 1.0, 6.0, ((0, 8), (1, 4)), jnp.float32)
    return dict(inputs=inputs, cotangent=cotangent, filters=filters)


def reference(inputs, cotangent, filters):
    scale = 1.0 / math.sqrt(2.0 * SEQ_LEN)
    filter_spectrum = jnp.fft.fft(filters, axis=0)
    effective = filter_spectrum + jnp.conj(filter_spectrum[:, ::-1])
    grads = []
    cross = jnp.zeros_like(filter_spectrum)
    for index in range(SEQS):
        inputs_spectrum = jnp.fft.fft(inputs[index], axis=0)
        cotangent_spectrum = jnp.fft.fft(cotangent[index], axis=0)
        input_spec = jnp.conj(effective) * cotangent_spectrum
        grads.append(jnp.real(jnp.fft.ifft(input_spec, axis=0)) * scale)
        cross = cross + cotangent_spectrum * jnp.conj(inputs_spectrum)
    filter_spec = cross + jnp.conj(cross[:, ::-1])
    filter_grad = jnp.real(jnp.fft.ifft(filter_spec, axis=0)) * scale
    input_grad = jnp.stack(grads, axis=0)
    return (input_grad.astype(jnp.float32), filter_grad.astype(jnp.float32))
```

```python
import functools
import math

import jax
import jax.numpy as jnp
import ml_dtypes
import numpy as np
from jax import lax
from jax.experimental import pallas as pl
from jax.experimental.pallas import tpu as pltpu
from jax.sharding import PartitionSpec as P

MESH = pl.DeviceIdType.MESH


def plus(left, right):
    if left is None:
        return right
    return left if right is None else left + right


def minus(left, right):
    if right is None:
        return left
    return -right if left is None else left - right


def turn(value, cos, sin):
    real, imag = value
    if imag is None:
        return (real * cos, real * sin)
    return (real * cos - imag * sin, real * sin + imag * cos)


def real_forward(items):
    n = len(items)
    if n == 1:
        return [(items[0], None)]
    even, odd = real_forward(items[0::2]), real_forward(items[1::2])
    out = [None] * (n // 2 + 1)
    out[0] = (even[0][0] + odd[0][0], None)
    out[n // 2] = (even[0][0] - odd[0][0], None)
    for k in range(1, n // 4 + 1):
        if 4 * k == n:
            out[k] = (even[k][0], -odd[k][0])
            continue
        angle = -2.0 * math.pi * k / n
        turned = turn(odd[k], math.cos(angle), math.sin(angle))
        out[k] = (plus(even[k][0], turned[0]), plus(even[k][1], turned[1]))
        out[n // 2 - k] = (minus(even[k][0], turned[0]), minus(turned[1], even[k][1]))
    return out


def real_inverse(items, n):
    if n == 1:
        return [items[0][0]]
    first, last = items[0][0], items[n // 2][0]
    if n == 2:
        return [first + last, first - last]
    even, odd = [(first + last, None)], [(first - last, None)]
    for k in range(1, n // 4 + 1):
        real, imag = items[k]
        if 4 * k == n:
            even.append((2.0 * real, None))
            odd.append((-2.0 * imag, None))
            continue
        far_real, far_imag = items[n // 2 - k]
        angle = 2.0 * math.pi * k / n
        even.append((real + far_real, imag - far_imag))
        odd.append(turn((real - far_real, imag + far_imag), math.cos(angle), math.sin(angle)))
    out = [None] * n
    out[0::2] = real_inverse(even, n // 2)
    out[1::2] = real_inverse(odd, n // 2)
    return out


def split(value):
    high = value.astype(jnp.bfloat16)
    return high, (value - high.astype(jnp.float32)).astype(jnp.bfloat16)


def product(value, table_hi, table_lo):
    high, low = split(value)
    dot = functools.partial(jnp.dot, preferred_element_type=jnp.float32)
    return dot(high, table_hi) + (dot(low, table_hi) + dot(high, table_lo))


def kernel(
    n, nch, seqs, factor,
    x_ref, g_ref, f_ref, hi_ref, lo_ref, cos_ref, sin_ref,
    dx_ref, df_ref,
    send_f, send_d, recv_f, recv_d, back_send, back_recv,
    lhs, spec, eff, cross, mirror, flipped,
    fwd_send, fwd_recv, ret_send, ret_recv, pair_send, pair_recv,
):
    me = lax.axis_index("ctx")
    ch = lax.axis_index("ch")
    partner = nch - 1 - ch
    upper = (2 * ch) // nch
    width = x_ref.shape[1]
    rows = x_ref.shape[2] // n
    half = n // 2

    def chunk(owner):
        return owner + upper * (n - 1 - 2 * owner)

    def peer(step):
        return lax.rem(me + step, n)

    def to_filter(other):
        return pltpu.make_async_remote_copy(
            src_ref=send_f.at[chunk(other)], dst_ref=recv_f.at[me],
            send_sem=fwd_send.at[seqs, other], recv_sem=fwd_recv.at[seqs, me],
            device_id={"ctx": other}, device_id_type=MESH,
        )

    def from_filter(other):
        return pltpu.make_async_remote_copy(
            src_ref=send_f.at[chunk(other)], dst_ref=recv_f.at[other],
            send_sem=fwd_send.at[seqs, other], recv_sem=fwd_recv.at[seqs, other],
            device_id={"ctx": other}, device_id_type=MESH,
        )

    def to_data(b, other):
        return pltpu.make_async_remote_copy(
            src_ref=send_d.at[b, chunk(other)], dst_ref=recv_d.at[b, me],
            send_sem=fwd_send.at[b, other], recv_sem=fwd_recv.at[b, me],
            device_id={"ctx": other}, device_id_type=MESH,
        )

    def from_data(b, other):
        return pltpu.make_async_remote_copy(
            src_ref=send_d.at[b, chunk(other)], dst_ref=recv_d.at[b, other],
            send_sem=fwd_send.at[b, other], recv_sem=fwd_recv.at[b, other],
            device_id={"ctx": other}, device_id_type=MESH,
        )

    def to_back(b, other):
        return pltpu.make_async_remote_copy(
            src_ref=back_send.at[b, other], dst_ref=back_recv.at[b, chunk(me)],
            send_sem=ret_send.at[b, other], recv_sem=ret_recv.at[b, me],
            device_id={"ctx": other}, device_id_type=MESH,
        )

    def from_back(b, other):
        return pltpu.make_async_remote_copy(
            src_ref=back_send.at[b, other], dst_ref=back_recv.at[b, chunk(other)],
            send_sem=ret_send.at[b, other], recv_sem=ret_recv.at[b, other],
            device_id={"ctx": other}, device_id_type=MESH,
        )

    def to_pair(which, source):
        return pltpu.make_async_remote_copy(
            src_ref=source, dst_ref=mirror.at[which],
            send_sem=pair_send.at[which], recv_sem=pair_recv.at[which],
            device_id={"ch": partner}, device_id_type=MESH,
        )

    def each_peer(act):
        @pl.loop(1, n)
        def _(step):
            act(peer(step))

    def forward(arrays, count):
        for p, (real, imag) in enumerate(real_forward(arrays)):
            if p > 0:
                cos, sin = cos_ref[p : p + 1, :], sin_ref[p : p + 1, :]
                real, imag = turn((real, imag), cos, -sin)
            lhs[p, :count, :width] = real
            lhs[p, :count, width:] = jnp.zeros_like(real) if imag is None else imag
        flat = lhs[:, :count, :].reshape((half + 1) * count, 2 * width)
        out = product(flat, hi_ref[...], lo_ref[...])
        spec[:, :count, :] = out.reshape(half + 1, count, 2 * width)

    def inverse(b):
        flat = lhs[:, :rows, :].reshape((half + 1) * rows, 2 * width)
        out = product(flat, hi_ref[...], lo_ref[...])
        out = out.reshape(half + 1, rows, 2 * width) * factor
        items = []
        for p in range(half + 1):
            value = (out[p, :, :width], -out[p, :, width:])
            if p > 0:
                cos, sin = cos_ref[p : p + 1, :], sin_ref[p : p + 1, :]
                value = turn(value, cos, sin)
            items.append(value)
        for i, block in enumerate(real_inverse(items, n)):
            back_send[b, i] = block
        back_recv[b, chunk(me)] = back_send[b, me]
        each_peer(lambda other: to_back(b, other).start())

    def add_mirror(which, target):
        for r in range(rows):
            flipped[:, r : r + 1, :] = mirror[which, :, rows - 1 - r : rows - r, :]
        target[:, :, :width] += flipped[:, :, :width]
        target[:, :, width:] -= flipped[:, :, width:]

    barrier = pltpu.get_barrier_semaphore()
    each_peer(
        lambda other: pl.semaphore_signal(
            barrier, inc=1, device_id={"ctx": other}, device_id_type=MESH
        )
    )
    pl.semaphore_signal(barrier, inc=1, device_id={"ch": partner}, device_id_type=MESH)
    send_f[...] = f_ref[...].T.reshape(n, rows, width)
    pl.semaphore_wait(barrier, n)

    each_peer(lambda other: to_filter(other).start())
    recv_f[me] = send_f[chunk(me)]

    @pl.loop(0, seqs)
    def _(b):
        send_d[b, :, 0] = g_ref[b].T.reshape(n, rows, width)
        send_d[b, :, 1] = x_ref[b].T.reshape(n, rows, width)
        each_peer(lambda other: to_data(b, other).start())
        recv_d[b, me] = send_d[b, chunk(me)]

    each_peer(lambda other: from_filter(other).wait_recv())
    forward([recv_f[i] for i in range(n)], rows)
    eff[...] = spec[:, :rows, :]
    swap_f = to_pair(0, eff)
    swap_f.start()
    cross[...] = jnp.zeros_like(cross)
    swap_f.wait()
    add_mirror(0, eff)

    @pl.loop(0, seqs)
    def _(b):
        each_peer(lambda other: from_data(b, other).wait_recv())
        forward([recv_d[b, i].reshape(2 * rows, width) for i in range(n)], 2 * rows)
        g_re, g_im = spec[:, :rows, :width], spec[:, :rows, width:]
        x_re, x_im = spec[:, rows:, :width], spec[:, rows:, width:]
        cross[:, :, :width] += g_re * x_re + g_im * x_im
        cross[:, :, width:] += g_im * x_re - g_re * x_im
        e_re, e_im = eff[:, :, :width], eff[:, :, width:]
        lhs[:, :rows, :width] = e_re * g_re + e_im * g_im
        lhs[:, :rows, width:] = e_im * g_re - e_re * g_im
        inverse(b)

    swap_c = to_pair(1, cross)
    swap_c.start()
    swap_c.wait()
    add_mirror(1, cross)
    lhs[:, :rows, :width] = cross[:, :, :width]
    lhs[:, :rows, width:] = -cross[:, :, width:]
    inverse(seqs)

    @pl.loop(0, seqs)
    def _(b):
        each_peer(lambda other: from_back(b, other).wait_recv())
        dx_ref[b] = back_recv[b].reshape(n * rows, width).T

    each_peer(lambda other: from_back(seqs, other).wait_recv())
    df_ref[...] = back_recv[seqs].reshape(n * rows, width).T

    each_peer(lambda other: to_filter(other).wait_send())

    @pl.loop(0, seqs)
    def _(b):
        each_peer(lambda other: to_data(b, other).wait_send())

    @pl.loop(0, seqs + 1)
    def _(b):
        each_peer(lambda other: to_back(b, other).wait_send())


def tables(n, width):
    period = n * width
    turns = np.outer(np.arange(width), np.arange(width)) % width
    angle = turns * (2.0 * math.pi / width)
    cos, sin = np.cos(angle), np.sin(angle)
    table = np.block([[cos, -sin], [sin, cos]]).astype(np.float32)
    high = table.astype(ml_dtypes.bfloat16)
    low = (table - high.astype(np.float32)).astype(ml_dtypes.bfloat16)
    angle = np.outer(np.arange(n // 2 + 1), np.arange(width)) * (2.0 * math.pi / period)
    return high, low, np.cos(angle).astype(np.float32), np.sin(angle).astype(np.float32)


def body(n, nch, inputs, cotangent, filters):
    seqs, width, channels = inputs.shape
    rows = channels // n
    half = n // 2
    period = n * width
    factor = 1.0 / (period * math.sqrt(2.0 * period))
    high, low, cos, sin = (jnp.asarray(value) for value in tables(n, width))
    vmem = pl.BlockSpec(memory_space=pltpu.VMEM)
    real = jnp.float32
    dma = pltpu.SemaphoreType.DMA
    return tuple(pl.pallas_call(
        functools.partial(kernel, n, nch, seqs, factor),
        out_shape=(
            jax.ShapeDtypeStruct(inputs.shape, real),
            jax.ShapeDtypeStruct(filters.shape, real),
        ),
        in_specs=[vmem] * 7,
        out_specs=(vmem, vmem),
        scratch_shapes=[
            pltpu.VMEM((n, rows, width), real),
            pltpu.VMEM((seqs, n, 2, rows, width), real),
            pltpu.VMEM((n, rows, width), real),
            pltpu.VMEM((seqs, n, 2, rows, width), real),
            pltpu.VMEM((seqs + 1, n, rows, width), real),
            pltpu.VMEM((seqs + 1, n, rows, width), real),
            pltpu.VMEM((half + 1, 2 * rows, 2 * width), real),
            pltpu.VMEM((half + 1, 2 * rows, 2 * width), real),
            pltpu.VMEM((half + 1, rows, 2 * width), real),
            pltpu.VMEM((half + 1, rows, 2 * width), real),
            pltpu.VMEM((2, half + 1, rows, 2 * width), real),
            pltpu.VMEM((half + 1, rows, 2 * width), real),
            dma((seqs + 1, n)), dma((seqs + 1, n)),
            dma((seqs + 1, n)), dma((seqs + 1, n)),
            dma((2,)), dma((2,)),
        ],
        compiler_params=pltpu.CompilerParams(
            collective_id=0, has_side_effects=True, vmem_limit_bytes=56 * 2**20
        ),
    )(inputs, cotangent, filters, high, low, cos, sin))


def solution(mesh):
    in_specs = (P(None, "ctx", "ch"), P(None, "ctx", "ch"), P("ctx", "ch"))
    out_specs = (P(None, "ctx", "ch"), P("ctx", "ch"))
    run = functools.partial(body, mesh.shape["ctx"], mesh.shape["ch"])
    return jax.shard_map(run, mesh=mesh, in_specs=in_specs, out_specs=out_specs, check_vma=False)
```

```python
import functools
import math

import jax
import jax.numpy as jnp
import ml_dtypes
import numpy as np
from jax import lax
from jax.experimental import pallas as pl
from jax.experimental.pallas import tpu as pltpu
from jax.sharding import PartitionSpec as P

MESH = pl.DeviceIdType.MESH


def plus(left, right):
    if left is None:
        return right
    return left if right is None else left + right


def minus(left, right):
    if right is None:
        return left
    return -right if left is None else left - right


def turn(value, cos, sin):
    real, imag = value
    if imag is None:
        return (real * cos, real * sin)
    return (real * cos - imag * sin, real * sin + imag * cos)


def real_forward(items):
    n = len(items)
    if n == 1:
        return [(items[0], None)]
    even, odd = real_forward(items[0::2]), real_forward(items[1::2])
    out = [None] * (n // 2 + 1)
    out[0] = (even[0][0] + odd[0][0], None)
    out[n // 2] = (even[0][0] - odd[0][0], None)
    for k in range(1, n // 4 + 1):
        if 4 * k == n:
            out[k] = (even[k][0], -odd[k][0])
            continue
        angle = -2.0 * math.pi * k / n
        turned = turn(odd[k], math.cos(angle), math.sin(angle))
        out[k] = (plus(even[k][0], turned[0]), plus(even[k][1], turned[1]))
        out[n // 2 - k] = (minus(even[k][0], turned[0]), minus(turned[1], even[k][1]))
    return out


def real_inverse(items, n):
    if n == 1:
        return [items[0][0]]
    first, last = items[0][0], items[n // 2][0]
    if n == 2:
        return [first + last, first - last]
    even, odd = [(first + last, None)], [(first - last, None)]
    for k in range(1, n // 4 + 1):
        real, imag = items[k]
        if 4 * k == n:
            even.append((2.0 * real, None))
            odd.append((-2.0 * imag, None))
            continue
        far_real, far_imag = items[n // 2 - k]
        angle = 2.0 * math.pi * k / n
        even.append((real + far_real, imag - far_imag))
        odd.append(turn((real - far_real, imag + far_imag), math.cos(angle), math.sin(angle)))
    out = [None] * n
    out[0::2] = real_inverse(even, n // 2)
    out[1::2] = real_inverse(odd, n // 2)
    return out


def split(value):
    high = value.astype(jnp.bfloat16)
    return high, (value - high.astype(jnp.float32)).astype(jnp.bfloat16)


def product(value, table_hi, table_lo):
    high, low = split(value)
    dot = functools.partial(jnp.dot, preferred_element_type=jnp.float32)
    return dot(high, table_hi) + (dot(low, table_hi) + dot(high, table_lo))


def kernel(
    n, nch, seqs, factor,
    x_hbm, g_hbm, f_hbm, hi_hbm, lo_hbm, cos_hbm, sin_hbm,
    dx_ref, df_ref,
    x_ref, g_ref, f_ref, hi_ref, lo_ref, cos_ref, sin_ref,
    send_f, send_d, recv_f, recv_d, back_send, back_recv,
    lhs, spec, eff, cross, mirror, flipped,
    fwd_send, fwd_recv, ret_send, ret_recv, pair_send, pair_recv, load_sem, table_sem,
):
    me = lax.axis_index("ctx")
    ch = lax.axis_index("ch")
    partner = nch - 1 - ch
    upper = (2 * ch) // nch
    width = x_ref.shape[1]
    rows = x_ref.shape[2] // n
    half = n // 2

    def chunk(owner):
        return owner + upper * (n - 1 - 2 * owner)

    def peer(step):
        mask = lax.rem(step + half - 2, n - 1) + 1
        other = me
        for bit in range(n.bit_length() - 1):
            weight = 2**bit
            other = other + lax.rem(mask // weight, 2) * weight * (1 - 2 * lax.rem(me // weight, 2))
        return other

    def load(b, which, source, target):
        return pltpu.make_async_copy(source.at[b], target.at[b], load_sem.at[b, which])

    def table(which, source, target):
        return pltpu.make_async_copy(source, target, table_sem.at[which])

    def to_filter(other):
        return pltpu.make_async_remote_copy(
            src_ref=send_f.at[chunk(other)], dst_ref=recv_f.at[me],
            send_sem=fwd_send.at[seqs, other], recv_sem=fwd_recv.at[seqs, me],
            device_id={"ctx": other}, device_id_type=MESH,
        )

    def from_filter(other):
        return pltpu.make_async_remote_copy(
            src_ref=send_f.at[chunk(other)], dst_ref=recv_f.at[other],
            send_sem=fwd_send.at[seqs, other], recv_sem=fwd_recv.at[seqs, other],
            device_id={"ctx": other}, device_id_type=MESH,
        )

    def to_data(b, other):
        return pltpu.make_async_remote_copy(
            src_ref=send_d.at[b, chunk(other)], dst_ref=recv_d.at[b, me],
            send_sem=fwd_send.at[b, other], recv_sem=fwd_recv.at[b, me],
            device_id={"ctx": other}, device_id_type=MESH,
        )

    def from_data(b, other):
        return pltpu.make_async_remote_copy(
            src_ref=send_d.at[b, chunk(other)], dst_ref=recv_d.at[b, other],
            send_sem=fwd_send.at[b, other], recv_sem=fwd_recv.at[b, other],
            device_id={"ctx": other}, device_id_type=MESH,
        )

    def to_back(b, other):
        return pltpu.make_async_remote_copy(
            src_ref=back_send.at[b, other], dst_ref=back_recv.at[b, chunk(me)],
            send_sem=ret_send.at[b, other], recv_sem=ret_recv.at[b, me],
            device_id={"ctx": other}, device_id_type=MESH,
        )

    def from_back(b, other):
        return pltpu.make_async_remote_copy(
            src_ref=back_send.at[b, other], dst_ref=back_recv.at[b, chunk(other)],
            send_sem=ret_send.at[b, other], recv_sem=ret_recv.at[b, other],
            device_id={"ctx": other}, device_id_type=MESH,
        )

    def to_pair(which, source):
        return pltpu.make_async_remote_copy(
            src_ref=source, dst_ref=mirror.at[which],
            send_sem=pair_send.at[which], recv_sem=pair_recv.at[which],
            device_id={"ch": partner}, device_id_type=MESH,
        )

    def each_peer(act):
        @pl.loop(1, n)
        def _(step):
            act(peer(step))

    def forward(arrays, count):
        for p, (real, imag) in enumerate(real_forward(arrays)):
            if p > 0:
                cos, sin = cos_ref[p : p + 1, :], sin_ref[p : p + 1, :]
                real, imag = turn((real, imag), cos, -sin)
            lhs[p, :count, :width] = real
            lhs[p, :count, width:] = jnp.zeros_like(real) if imag is None else imag
        flat = lhs[:, :count, :].reshape((half + 1) * count, 2 * width)
        out = product(flat, hi_ref[...], lo_ref[...])
        spec[:, :count, :] = out.reshape(half + 1, count, 2 * width)

    def inverse(b):
        flat = lhs[:, :rows, :].reshape((half + 1) * rows, 2 * width)
        out = product(flat, hi_ref[...], lo_ref[...])
        out = out.reshape(half + 1, rows, 2 * width) * factor
        items = []
        for p in range(half + 1):
            value = (out[p, :, :width], -out[p, :, width:])
            if p > 0:
                cos, sin = cos_ref[p : p + 1, :], sin_ref[p : p + 1, :]
                value = turn(value, cos, sin)
            items.append(value)
        for i, block in enumerate(real_inverse(items, n)):
            back_send[b, i] = block
        back_recv[b, chunk(me)] = back_send[b, me]

    def give_back(b):
        each_peer(lambda other: to_back(b, other).start())

    def add_mirror(which, target):
        for r in range(rows):
            flipped[:, r : r + 1, :] = mirror[which, :, rows - 1 - r : rows - r, :]
        target[:, :, :width] += flipped[:, :, :width]
        target[:, :, width:] -= flipped[:, :, width:]

    filter_load = table(0, f_hbm, f_ref)
    filter_load.start()

    @pl.loop(0, seqs)
    def _(b):
        load(b, 0, g_hbm, g_ref).start()
        load(b, 1, x_hbm, x_ref).start()

    table_loads = [
        table(1, hi_hbm, hi_ref), table(2, lo_hbm, lo_ref),
        table(3, cos_hbm, cos_ref), table(4, sin_hbm, sin_ref),
    ]
    for copy in table_loads:
        copy.start()

    barrier = pltpu.get_barrier_semaphore()
    each_peer(
        lambda other: pl.semaphore_signal(
            barrier, inc=1, device_id={"ctx": other}, device_id_type=MESH
        )
    )
    pl.semaphore_signal(barrier, inc=1, device_id={"ch": partner}, device_id_type=MESH)
    filter_load.wait()
    send_f[...] = f_ref[...].T.reshape(n, rows, width)
    pl.semaphore_wait(barrier, n)

    each_peer(lambda other: to_filter(other).start())
    recv_f[me] = send_f[chunk(me)]

    @pl.loop(0, seqs)
    def _(b):
        load(b, 0, g_hbm, g_ref).wait()
        load(b, 1, x_hbm, x_ref).wait()
        send_d[b, :, 0] = g_ref[b].T.reshape(n, rows, width)
        send_d[b, :, 1] = x_ref[b].T.reshape(n, rows, width)
        each_peer(lambda other: to_data(b, other).start())
        recv_d[b, me] = send_d[b, chunk(me)]

    for copy in table_loads:
        copy.wait()
    each_peer(lambda other: from_filter(other).wait_recv())
    forward([recv_f[i] for i in range(n)], rows)
    eff[...] = spec[:, :rows, :]
    swap_f = to_pair(0, eff)
    swap_f.start()
    cross[...] = jnp.zeros_like(cross)
    swap_f.wait()
    add_mirror(0, eff)

    def gradient(b):
        each_peer(lambda other: from_data(b, other).wait_recv())
        forward([recv_d[b, i].reshape(2 * rows, width) for i in range(n)], 2 * rows)
        g_re, g_im = spec[:, :rows, :width], spec[:, :rows, width:]
        x_re, x_im = spec[:, rows:, :width], spec[:, rows:, width:]
        cross[:, :, :width] += g_re * x_re + g_im * x_im
        cross[:, :, width:] += g_im * x_re - g_re * x_im
        e_re, e_im = eff[:, :, :width], eff[:, :, width:]
        lhs[:, :rows, :width] = e_re * g_re + e_im * g_im
        lhs[:, :rows, width:] = e_im * g_re - e_re * g_im
        inverse(b)

    pl.loop(0, seqs - 1)(gradient)
    each_peer(lambda other: to_filter(other).wait_send())

    @pl.loop(0, seqs)
    def _(b):
        each_peer(lambda other: to_data(b, other).wait_send())

    pl.loop(0, seqs - 1)(give_back)
    gradient(seqs - 1)
    swap_c = to_pair(1, cross)
    swap_c.start()
    give_back(seqs - 1)
    swap_c.wait()
    add_mirror(1, cross)
    lhs[:, :rows, :width] = cross[:, :, :width]
    lhs[:, :rows, width:] = -cross[:, :, width:]
    inverse(seqs)
    give_back(seqs)

    @pl.loop(0, seqs)
    def _(b):
        each_peer(lambda other: from_back(b, other).wait_recv())
        dx_ref[b] = back_recv[b].reshape(n * rows, width).T

    each_peer(lambda other: from_back(seqs, other).wait_recv())
    df_ref[...] = back_recv[seqs].reshape(n * rows, width).T

    @pl.loop(0, seqs + 1)
    def _(b):
        each_peer(lambda other: to_back(b, other).wait_send())


def tables(n, width):
    period = n * width
    turns = np.outer(np.arange(width), np.arange(width)) % width
    angle = turns * (2.0 * math.pi / width)
    cos, sin = np.cos(angle), np.sin(angle)
    table = np.block([[cos, -sin], [sin, cos]]).astype(np.float32)
    high = table.astype(ml_dtypes.bfloat16)
    low = (table - high.astype(np.float32)).astype(ml_dtypes.bfloat16)
    angle = np.outer(np.arange(n // 2 + 1), np.arange(width)) * (2.0 * math.pi / period)
    return high, low, np.cos(angle).astype(np.float32), np.sin(angle).astype(np.float32)


def body(n, nch, inputs, cotangent, filters):
    seqs, width, channels = inputs.shape
    rows = channels // n
    half = n // 2
    period = n * width
    factor = 1.0 / (period * math.sqrt(2.0 * period))
    high, low, cos, sin = (jnp.asarray(value) for value in tables(n, width))
    vmem = pl.BlockSpec(memory_space=pltpu.VMEM)
    anywhere = pl.BlockSpec(memory_space=pl.ANY)
    real = jnp.float32
    dma = pltpu.SemaphoreType.DMA
    return tuple(pl.pallas_call(
        functools.partial(kernel, n, nch, seqs, factor),
        out_shape=(
            jax.ShapeDtypeStruct(inputs.shape, real),
            jax.ShapeDtypeStruct(filters.shape, real),
        ),
        in_specs=[anywhere] * 7,
        out_specs=(vmem, vmem),
        scratch_shapes=[
            pltpu.VMEM(inputs.shape, real),
            pltpu.VMEM(inputs.shape, real),
            pltpu.VMEM(filters.shape, real),
            pltpu.VMEM(high.shape, high.dtype),
            pltpu.VMEM(low.shape, low.dtype),
            pltpu.VMEM(cos.shape, real),
            pltpu.VMEM(sin.shape, real),
            pltpu.VMEM((n, rows, width), real),
            pltpu.VMEM((seqs, n, 2, rows, width), real),
            pltpu.VMEM((n, rows, width), real),
            pltpu.VMEM((seqs, n, 2, rows, width), real),
            pltpu.VMEM((seqs + 1, n, rows, width), real),
            pltpu.VMEM((seqs + 1, n, rows, width), real),
            pltpu.VMEM((half + 1, 2 * rows, 2 * width), real),
            pltpu.VMEM((half + 1, 2 * rows, 2 * width), real),
            pltpu.VMEM((half + 1, rows, 2 * width), real),
            pltpu.VMEM((half + 1, rows, 2 * width), real),
            pltpu.VMEM((2, half + 1, rows, 2 * width), real),
            pltpu.VMEM((half + 1, rows, 2 * width), real),
            dma((seqs + 1, n)), dma((seqs + 1, n)),
            dma((seqs + 1, n)), dma((seqs + 1, n)),
            dma((2,)), dma((2,)), dma((seqs, 2)), dma((5,)),
        ],
        compiler_params=pltpu.CompilerParams(
            collective_id=0, has_side_effects=True, vmem_limit_bytes=56 * 2**20
        ),
    )(inputs, cotangent, filters, high, low, cos, sin))


def solution(mesh):
    in_specs = (P(None, "ctx", "ch"), P(None, "ctx", "ch"), P("ctx", "ch"))
    out_specs = (P(None, "ctx", "ch"), P("ctx", "ch"))
    run = functools.partial(body, mesh.shape["ctx"], mesh.shape["ch"])
    return jax.shard_map(run, mesh=mesh, in_specs=in_specs, out_specs=out_specs, check_vma=False)
```

```python
import functools
import math

import jax
import jax.numpy as jnp
import ml_dtypes
import numpy as np
from jax import lax
from jax.experimental import pallas as pl
from jax.experimental.pallas import tpu as pltpu
from jax.sharding import PartitionSpec as P

MESH = pl.DeviceIdType.MESH


def plus(left, right):
    if left is None:
        return right
    return left if right is None else left + right


def minus(left, right):
    if right is None:
        return left
    return -right if left is None else left - right


def turn(value, cos, sin):
    real, imag = value
    if imag is None:
        return (real * cos, real * sin)
    return (real * cos - imag * sin, real * sin + imag * cos)


def real_forward(items):
    n = len(items)
    if n == 1:
        return [(items[0], None)]
    even, odd = real_forward(items[0::2]), real_forward(items[1::2])
    out = [None] * (n // 2 + 1)
    out[0] = (even[0][0] + odd[0][0], None)
    out[n // 2] = (even[0][0] - odd[0][0], None)
    for k in range(1, n // 4 + 1):
        if 4 * k == n:
            out[k] = (even[k][0], -odd[k][0])
            continue
        angle = -2.0 * math.pi * k / n
        turned = turn(odd[k], math.cos(angle), math.sin(angle))
        out[k] = (plus(even[k][0], turned[0]), plus(even[k][1], turned[1]))
        out[n // 2 - k] = (minus(even[k][0], turned[0]), minus(turned[1], even[k][1]))
    return out


def real_inverse(items, n):
    if n == 1:
        return [items[0][0]]
    first, last = items[0][0], items[n // 2][0]
    if n == 2:
        return [first + last, first - last]
    even, odd = [(first + last, None)], [(first - last, None)]
    for k in range(1, n // 4 + 1):
        real, imag = items[k]
        if 4 * k == n:
            even.append((2.0 * real, None))
            odd.append((-2.0 * imag, None))
            continue
        far_real, far_imag = items[n // 2 - k]
        angle = 2.0 * math.pi * k / n
        even.append((real + far_real, imag - far_imag))
        odd.append(turn((real - far_real, imag + far_imag), math.cos(angle), math.sin(angle)))
    out = [None] * n
    out[0::2] = real_inverse(even, n // 2)
    out[1::2] = real_inverse(odd, n // 2)
    return out


def split(value):
    high = value.astype(jnp.bfloat16)
    return high, (value - high.astype(jnp.float32)).astype(jnp.bfloat16)


def product(value, table_hi, table_lo):
    high, low = split(value)
    dot = functools.partial(jnp.dot, preferred_element_type=jnp.float32)
    return dot(high, table_hi) + (dot(low, table_hi) + dot(high, table_lo))


def kernel(
    n, nch, seqs, factor,
    x_hbm, g_hbm, f_hbm, hi_hbm, lo_hbm, cos_hbm, sin_hbm,
    dx_ref, df_ref,
    x_ref, g_ref, f_ref, hi_ref, lo_ref, cos_ref, sin_ref,
    send_f, send_d, recv_f, recv_d, back_send, back_recv,
    lhs, spec, eff, cross, mirror, flipped,
    fwd_send, fwd_recv, ret_send, ret_recv, pair_send, pair_recv, load_sem, table_sem,
):
    me = lax.axis_index("ctx")
    ch = lax.axis_index("ch")
    partner = nch - 1 - ch
    upper = (2 * ch) // nch
    width = x_ref.shape[1]
    rows = x_ref.shape[2] // n
    half = n // 2

    def chunk(owner):
        return owner + upper * (n - 1 - 2 * owner)

    def peer(step):
        mask = lax.rem(step + half - 2, n - 1) + 1
        other = me
        for bit in range(n.bit_length() - 1):
            weight = 2**bit
            other = other + lax.rem(mask // weight, 2) * weight * (1 - 2 * lax.rem(me // weight, 2))
        return other

    def load(b, which, source, target):
        return pltpu.make_async_copy(source.at[b], target.at[b], load_sem.at[b, which])

    def table(which, source, target):
        return pltpu.make_async_copy(source, target, table_sem.at[which])

    def to_filter(other):
        return pltpu.make_async_remote_copy(
            src_ref=send_f.at[chunk(other)], dst_ref=recv_f.at[me],
            send_sem=fwd_send.at[seqs, other], recv_sem=fwd_recv.at[seqs, me],
            device_id={"ctx": other}, device_id_type=MESH,
        )

    def from_filter(other):
        return pltpu.make_async_remote_copy(
            src_ref=send_f.at[chunk(other)], dst_ref=recv_f.at[other],
            send_sem=fwd_send.at[seqs, other], recv_sem=fwd_recv.at[seqs, other],
            device_id={"ctx": other}, device_id_type=MESH,
        )

    def to_data(b, other):
        return pltpu.make_async_remote_copy(
            src_ref=send_d.at[b, chunk(other)], dst_ref=recv_d.at[b, me],
            send_sem=fwd_send.at[b, other], recv_sem=fwd_recv.at[b, me],
            device_id={"ctx": other}, device_id_type=MESH,
        )

    def from_data(b, other):
        return pltpu.make_async_remote_copy(
            src_ref=send_d.at[b, chunk(other)], dst_ref=recv_d.at[b, other],
            send_sem=fwd_send.at[b, other], recv_sem=fwd_recv.at[b, other],
            device_id={"ctx": other}, device_id_type=MESH,
        )

    def to_back(b, other):
        return pltpu.make_async_remote_copy(
            src_ref=back_send.at[b, other], dst_ref=back_recv.at[b, chunk(me)],
            send_sem=ret_send.at[b, other], recv_sem=ret_recv.at[b, me],
            device_id={"ctx": other}, device_id_type=MESH,
        )

    def from_back(b, other):
        return pltpu.make_async_remote_copy(
            src_ref=back_send.at[b, other], dst_ref=back_recv.at[b, chunk(other)],
            send_sem=ret_send.at[b, other], recv_sem=ret_recv.at[b, other],
            device_id={"ctx": other}, device_id_type=MESH,
        )

    def to_pair(which, source):
        return pltpu.make_async_remote_copy(
            src_ref=source, dst_ref=mirror.at[which],
            send_sem=pair_send.at[which], recv_sem=pair_recv.at[which],
            device_id={"ch": partner}, device_id_type=MESH,
        )

    def each_peer(act):
        @pl.loop(1, n)
        def _(step):
            act(peer(step))

    def forward(arrays, count):
        for p, (real, imag) in enumerate(real_forward(arrays)):
            if p > 0:
                cos, sin = cos_ref[p : p + 1, :], sin_ref[p : p + 1, :]
                real, imag = turn((real, imag), cos, -sin)
            lhs[p, :count, :width] = real
            lhs[p, :count, width:] = jnp.zeros_like(real) if imag is None else imag
        flat = lhs[:, :count, :].reshape((half + 1) * count, 2 * width)
        out = product(flat, hi_ref[...], lo_ref[...])
        spec[:, :count, :] = out.reshape(half + 1, count, 2 * width)

    def inverse(b):
        flat = lhs[:, :rows, :].reshape((half + 1) * rows, 2 * width)
        out = product(flat, hi_ref[...], lo_ref[...])
        out = out.reshape(half + 1, rows, 2 * width) * factor
        items = []
        for p in range(half + 1):
            value = (out[p, :, :width], -out[p, :, width:])
            if p > 0:
                cos, sin = cos_ref[p : p + 1, :], sin_ref[p : p + 1, :]
                value = turn(value, cos, sin)
            items.append(value)
        for i, block in enumerate(real_inverse(items, n)):
            back_send[b, i] = block
        back_recv[b, chunk(me)] = back_send[b, me]

    def give_back(b):
        each_peer(lambda other: to_back(b, other).start())

    def add_mirror(which, target):
        for r in range(rows):
            flipped[:, r : r + 1, :] = mirror[which, :, rows - 1 - r : rows - r, :]
        target[:, :, :width] += flipped[:, :, :width]
        target[:, :, width:] -= flipped[:, :, width:]

    filter_load = table(0, f_hbm, f_ref)
    filter_load.start()

    @pl.loop(0, seqs)
    def _(b):
        load(b, 0, g_hbm, g_ref).start()
        load(b, 1, x_hbm, x_ref).start()

    table_loads = [
        table(1, hi_hbm, hi_ref), table(2, lo_hbm, lo_ref),
        table(3, cos_hbm, cos_ref), table(4, sin_hbm, sin_ref),
    ]
    for copy in table_loads:
        copy.start()

    barrier = pltpu.get_barrier_semaphore()
    each_peer(
        lambda other: pl.semaphore_signal(
            barrier, inc=1, device_id={"ctx": other}, device_id_type=MESH
        )
    )
    pl.semaphore_signal(barrier, inc=1, device_id={"ch": partner}, device_id_type=MESH)
    filter_load.wait()
    send_f[...] = f_ref[...].T.reshape(n, rows, width)
    pl.semaphore_wait(barrier, n)

    each_peer(lambda other: to_filter(other).start())
    recv_f[me] = send_f[chunk(me)]

    @pl.loop(0, seqs)
    def _(b):
        load(b, 0, g_hbm, g_ref).wait()
        load(b, 1, x_hbm, x_ref).wait()
        send_d[b, :, 0] = g_ref[b].T.reshape(n, rows, width)
        send_d[b, :, 1] = x_ref[b].T.reshape(n, rows, width)
        each_peer(lambda other: to_data(b, other).start())
        recv_d[b, me] = send_d[b, chunk(me)]

    for copy in table_loads:
        copy.wait()
    each_peer(lambda other: from_filter(other).wait_recv())
    forward([recv_f[i] for i in range(n)], rows)
    eff[...] = spec[:, :rows, :]
    swap_f = to_pair(0, eff)
    swap_f.start()
    cross[...] = jnp.zeros_like(cross)
    swap_f.wait()
    add_mirror(0, eff)

    def gradient(b):
        each_peer(lambda other: from_data(b, other).wait_recv())
        forward([recv_d[b, i].reshape(2 * rows, width) for i in range(n)], 2 * rows)
        g_re, g_im = spec[:, :rows, :width], spec[:, :rows, width:]
        x_re, x_im = spec[:, rows:, :width], spec[:, rows:, width:]
        cross[:, :, :width] += g_re * x_re + g_im * x_im
        cross[:, :, width:] += g_im * x_re - g_re * x_im
        e_re, e_im = eff[:, :, :width], eff[:, :, width:]
        lhs[:, :rows, :width] = e_re * g_re + e_im * g_im
        lhs[:, :rows, width:] = e_im * g_re - e_re * g_im
        inverse(b)

    pl.loop(0, seqs - 1)(gradient)
    each_peer(lambda other: to_filter(other).wait_send())

    @pl.loop(0, seqs)
    def _(b):
        each_peer(lambda other: to_data(b, other).wait_send())

    pl.loop(0, seqs - 1)(give_back)
    gradient(seqs - 1)
    swap_c = to_pair(1, cross)
    swap_c.start()
    give_back(seqs - 1)
    swap_c.wait()
    add_mirror(1, cross)
    lhs[:, :rows, :width] = cross[:, :, :width]
    lhs[:, :rows, width:] = -cross[:, :, width:]
    inverse(seqs)
    give_back(seqs)

    @pl.loop(0, seqs)
    def _(b):
        each_peer(lambda other: from_back(b, other).wait_recv())
        dx_ref[b] = back_recv[b].reshape(n * rows, width).T

    each_peer(lambda other: from_back(seqs, other).wait_recv())
    df_ref[...] = back_recv[seqs].reshape(n * rows, width).T

    @pl.loop(0, seqs + 1)
    def _(b):
        each_peer(lambda other: to_back(b, other).wait_send())


def tables(n, width):
    period = n * width
    turns = np.outer(np.arange(width), np.arange(width)) % width
    angle = turns * (2.0 * math.pi / width)
    cos, sin = np.cos(angle), np.sin(angle)
    table = np.block([[cos, -sin], [sin, cos]]).astype(np.float32)
    high = table.astype(ml_dtypes.bfloat16)
    low = (table - high.astype(np.float32)).astype(ml_dtypes.bfloat16)
    angle = np.outer(np.arange(n // 2 + 1), np.arange(width)) * (2.0 * math.pi / period)
    return high, low, np.cos(angle).astype(np.float32), np.sin(angle).astype(np.float32)


def body(n, nch, inputs, cotangent, filters):
    seqs, width, channels = inputs.shape
    rows = channels // n
    half = n // 2
    period = n * width
    factor = 1.0 / (period * math.sqrt(2.0 * period))
    high, low, cos, sin = (jnp.asarray(value) for value in tables(n, width))
    vmem = pl.BlockSpec(memory_space=pltpu.VMEM)
    anywhere = pl.BlockSpec(memory_space=pl.ANY)
    real = jnp.float32
    dma = pltpu.SemaphoreType.DMA
    return tuple(pl.pallas_call(
        functools.partial(kernel, n, nch, seqs, factor),
        out_shape=(
            pltpu.VMEM(inputs.shape, real),
            pltpu.VMEM(filters.shape, real),
        ),
        in_specs=[anywhere] * 7,
        out_specs=(vmem, vmem),
        scratch_shapes=[
            pltpu.VMEM(inputs.shape, real),
            pltpu.VMEM(inputs.shape, real),
            pltpu.VMEM(filters.shape, real),
            pltpu.VMEM(high.shape, high.dtype),
            pltpu.VMEM(low.shape, low.dtype),
            pltpu.VMEM(cos.shape, real),
            pltpu.VMEM(sin.shape, real),
            pltpu.VMEM((n, rows, width), real),
            pltpu.VMEM((seqs, n, 2, rows, width), real),
            pltpu.VMEM((n, rows, width), real),
            pltpu.VMEM((seqs, n, 2, rows, width), real),
            pltpu.VMEM((seqs + 1, n, rows, width), real),
            pltpu.VMEM((seqs + 1, n, rows, width), real),
            pltpu.VMEM((half + 1, 2 * rows, 2 * width), real),
            pltpu.VMEM((half + 1, 2 * rows, 2 * width), real),
            pltpu.VMEM((half + 1, rows, 2 * width), real),
            pltpu.VMEM((half + 1, rows, 2 * width), real),
            pltpu.VMEM((2, half + 1, rows, 2 * width), real),
            pltpu.VMEM((half + 1, rows, 2 * width), real),
            dma((seqs + 1, n)), dma((seqs + 1, n)),
            dma((seqs + 1, n)), dma((seqs + 1, n)),
            dma((2,)), dma((2,)), dma((seqs, 2)), dma((5,)),
        ],
        compiler_params=pltpu.CompilerParams(
            collective_id=0, has_side_effects=True, vmem_limit_bytes=56 * 2**20
        ),
    )(inputs, cotangent, filters, high, low, cos, sin))


def solution(mesh):
    in_specs = (P(None, "ctx", "ch"), P(None, "ctx", "ch"), P("ctx", "ch"))
    out_specs = (P(None, "ctx", "ch"), P("ctx", "ch"))
    run = functools.partial(body, mesh.shape["ctx"], mesh.shape["ch"])
    return jax.shard_map(run, mesh=mesh, in_specs=in_specs, out_specs=out_specs, check_vma=False)
```

```python
import functools
import math

import jax
import jax.numpy as jnp
import ml_dtypes
import numpy as np
from jax import lax
from jax.experimental import pallas as pl
from jax.experimental.pallas import tpu as pltpu
from jax.sharding import PartitionSpec as P

MESH = pl.DeviceIdType.MESH


def plus(left, right):
    if left is None:
        return right
    return left if right is None else left + right


def minus(left, right):
    if right is None:
        return left
    return -right if left is None else left - right


def turn(value, cos, sin):
    real, imag = value
    if imag is None:
        return (real * cos, real * sin)
    return (real * cos - imag * sin, real * sin + imag * cos)


def real_forward(items):
    n = len(items)
    if n == 1:
        return [(items[0], None)]
    even, odd = real_forward(items[0::2]), real_forward(items[1::2])
    out = [None] * (n // 2 + 1)
    out[0] = (even[0][0] + odd[0][0], None)
    out[n // 2] = (even[0][0] - odd[0][0], None)
    for k in range(1, n // 4 + 1):
        if 4 * k == n:
            out[k] = (even[k][0], -odd[k][0])
            continue
        angle = -2.0 * math.pi * k / n
        turned = turn(odd[k], math.cos(angle), math.sin(angle))
        out[k] = (plus(even[k][0], turned[0]), plus(even[k][1], turned[1]))
        out[n // 2 - k] = (minus(even[k][0], turned[0]), minus(turned[1], even[k][1]))
    return out


def real_inverse(items, n):
    if n == 1:
        return [items[0][0]]
    first, last = items[0][0], items[n // 2][0]
    if n == 2:
        return [first + last, first - last]
    even, odd = [(first + last, None)], [(first - last, None)]
    for k in range(1, n // 4 + 1):
        real, imag = items[k]
        if 4 * k == n:
            even.append((2.0 * real, None))
            odd.append((-2.0 * imag, None))
            continue
        far_real, far_imag = items[n // 2 - k]
        angle = 2.0 * math.pi * k / n
        even.append((real + far_real, imag - far_imag))
        odd.append(turn((real - far_real, imag + far_imag), math.cos(angle), math.sin(angle)))
    out = [None] * n
    out[0::2] = real_inverse(even, n // 2)
    out[1::2] = real_inverse(odd, n // 2)
    return out


def split(value):
    high = value.astype(jnp.bfloat16)
    return high, (value - high.astype(jnp.float32)).astype(jnp.bfloat16)


def product(value, table_hi, table_lo):
    high, low = split(value)
    dot = functools.partial(jnp.dot, preferred_element_type=jnp.float32)
    return dot(high, table_hi) + (dot(low, table_hi) + dot(high, table_lo))


def kernel(
    n, nch, seqs, factor,
    x_hbm, g_hbm, f_hbm, hi_hbm, lo_hbm, cos_hbm, sin_hbm,
    dx_ref, df_ref,
    x_ref, g_ref, f_ref, hi_ref, lo_ref, cos_ref, sin_ref,
    send_f, send_d, recv_f, recv_d, back_send, back_recv,
    lhs, spec, eff, cross, mirror, flipped,
    fwd_send, fwd_recv, ret_send, ret_recv, pair_send, pair_recv, load_sem, table_sem,
):
    me = lax.axis_index("ctx")
    ch = lax.axis_index("ch")
    partner = nch - 1 - ch
    upper = (2 * ch) // nch
    width = x_ref.shape[1]
    rows = x_ref.shape[2] // n
    half = n // 2

    def chunk(owner):
        return owner + upper * (n - 1 - 2 * owner)

    def peer(step):
        mask = lax.rem(step + half - 2, n - 1) + 1
        other = me
        for bit in range(n.bit_length() - 1):
            weight = 2**bit
            other = other + lax.rem(mask // weight, 2) * weight * (1 - 2 * lax.rem(me // weight, 2))
        return other

    def load(b, which, source, target):
        return pltpu.make_async_copy(source.at[b], target.at[b], load_sem.at[b, which])

    def table(which, source, target):
        return pltpu.make_async_copy(source, target, table_sem.at[which])

    def to_filter(other):
        return pltpu.make_async_remote_copy(
            src_ref=send_f.at[chunk(other)], dst_ref=recv_f.at[me],
            send_sem=fwd_send.at[seqs, other], recv_sem=fwd_recv.at[seqs, me],
            device_id={"ctx": other}, device_id_type=MESH,
        )

    def from_filter(other):
        return pltpu.make_async_remote_copy(
            src_ref=send_f.at[chunk(other)], dst_ref=recv_f.at[other],
            send_sem=fwd_send.at[seqs, other], recv_sem=fwd_recv.at[seqs, other],
            device_id={"ctx": other}, device_id_type=MESH,
        )

    def to_data(b, other):
        return pltpu.make_async_remote_copy(
            src_ref=send_d.at[b, chunk(other)], dst_ref=recv_d.at[b, me],
            send_sem=fwd_send.at[b, other], recv_sem=fwd_recv.at[b, me],
            device_id={"ctx": other}, device_id_type=MESH,
        )

    def from_data(b, other):
        return pltpu.make_async_remote_copy(
            src_ref=send_d.at[b, chunk(other)], dst_ref=recv_d.at[b, other],
            send_sem=fwd_send.at[b, other], recv_sem=fwd_recv.at[b, other],
            device_id={"ctx": other}, device_id_type=MESH,
        )

    def to_back(b, other):
        return pltpu.make_async_remote_copy(
            src_ref=back_send.at[b, other], dst_ref=back_recv.at[b, chunk(me)],
            send_sem=ret_send.at[b, other], recv_sem=ret_recv.at[b, me],
            device_id={"ctx": other}, device_id_type=MESH,
        )

    def from_back(b, other):
        return pltpu.make_async_remote_copy(
            src_ref=back_send.at[b, other], dst_ref=back_recv.at[b, chunk(other)],
            send_sem=ret_send.at[b, other], recv_sem=ret_recv.at[b, other],
            device_id={"ctx": other}, device_id_type=MESH,
        )

    def to_pair(which, source):
        return pltpu.make_async_remote_copy(
            src_ref=source, dst_ref=mirror.at[which],
            send_sem=pair_send.at[which], recv_sem=pair_recv.at[which],
            device_id={"ch": partner}, device_id_type=MESH,
        )

    def each_peer(act):
        @pl.loop(1, n)
        def _(step):
            act(peer(step))

    def forward(arrays, count):
        for p, (real, imag) in enumerate(real_forward(arrays)):
            if p > 0:
                cos, sin = cos_ref[p : p + 1, :], sin_ref[p : p + 1, :]
                real, imag = turn((real, imag), cos, -sin)
            lhs[p, :count, :width] = real
            lhs[p, :count, width:] = jnp.zeros_like(real) if imag is None else imag
        flat = lhs[:, :count, :].reshape((half + 1) * count, 2 * width)
        out = product(flat, hi_ref[...], lo_ref[...])
        spec[:, :count, :] = out.reshape(half + 1, count, 2 * width)

    def inverse(b):
        flat = lhs[:, :rows, :].reshape((half + 1) * rows, 2 * width)
        out = product(flat, hi_ref[...], lo_ref[...])
        out = out.reshape(half + 1, rows, 2 * width) * factor
        items = []
        for p in range(half + 1):
            value = (out[p, :, :width], -out[p, :, width:])
            if p > 0:
                cos, sin = cos_ref[p : p + 1, :], sin_ref[p : p + 1, :]
                value = turn(value, cos, sin)
            items.append(value)
        for i, block in enumerate(real_inverse(items, n)):
            back_send[b, i] = block
        back_recv[b, chunk(me)] = back_send[b, me]

    def give_back(b):
        each_peer(lambda other: to_back(b, other).start())

    def add_mirror(which, target):
        for r in range(rows):
            flipped[:, r : r + 1, :] = mirror[which, :, rows - 1 - r : rows - r, :]
        target[:, :, :width] += flipped[:, :, :width]
        target[:, :, width:] -= flipped[:, :, width:]

    filter_load = table(0, f_hbm, f_ref)
    filter_load.start()

    barrier = pltpu.get_barrier_semaphore()
    each_peer(
        lambda other: pl.semaphore_signal(
            barrier, inc=1, device_id={"ctx": other}, device_id_type=MESH
        )
    )
    pl.semaphore_signal(barrier, inc=1, device_id={"ch": partner}, device_id_type=MESH)

    @pl.loop(0, seqs)
    def _(b):
        load(b, 0, g_hbm, g_ref).start()
        load(b, 1, x_hbm, x_ref).start()

    table_loads = [
        table(1, hi_hbm, hi_ref), table(2, lo_hbm, lo_ref),
        table(3, cos_hbm, cos_ref), table(4, sin_hbm, sin_ref),
    ]
    for copy in table_loads:
        copy.start()

    filter_load.wait()
    send_f[...] = f_ref[...].T.reshape(n, rows, width)
    pl.semaphore_wait(barrier, n)

    each_peer(lambda other: to_filter(other).start())
    recv_f[me] = send_f[chunk(me)]

    @pl.loop(0, seqs)
    def _(b):
        load(b, 0, g_hbm, g_ref).wait()
        load(b, 1, x_hbm, x_ref).wait()
        send_d[b, :, 0] = g_ref[b].T.reshape(n, rows, width)
        send_d[b, :, 1] = x_ref[b].T.reshape(n, rows, width)
        each_peer(lambda other: to_data(b, other).start())
        recv_d[b, me] = send_d[b, chunk(me)]

    for copy in table_loads:
        copy.wait()
    each_peer(lambda other: from_filter(other).wait_recv())
    forward([recv_f[i] for i in range(n)], rows)
    eff[...] = spec[:, :rows, :]
    swap_f = to_pair(0, eff)
    swap_f.start()
    cross[...] = jnp.zeros_like(cross)
    swap_f.wait()
    add_mirror(0, eff)

    def gradient(b):
        each_peer(lambda other: from_data(b, other).wait_recv())
        forward([recv_d[b, i].reshape(2 * rows, width) for i in range(n)], 2 * rows)
        g_re, g_im = spec[:, :rows, :width], spec[:, :rows, width:]
        x_re, x_im = spec[:, rows:, :width], spec[:, rows:, width:]
        cross[:, :, :width] += g_re * x_re + g_im * x_im
        cross[:, :, width:] += g_im * x_re - g_re * x_im
        e_re, e_im = eff[:, :, :width], eff[:, :, width:]
        lhs[:, :rows, :width] = e_re * g_re + e_im * g_im
        lhs[:, :rows, width:] = e_im * g_re - e_re * g_im
        inverse(b)

    pl.loop(0, seqs - 1)(gradient)
    each_peer(lambda other: to_filter(other).wait_send())

    @pl.loop(0, seqs)
    def _(b):
        each_peer(lambda other: to_data(b, other).wait_send())

    pl.loop(0, seqs - 1)(give_back)
    gradient(seqs - 1)
    swap_c = to_pair(1, cross)
    swap_c.start()
    give_back(seqs - 1)
    swap_c.wait()
    add_mirror(1, cross)
    lhs[:, :rows, :width] = cross[:, :, :width]
    lhs[:, :rows, width:] = -cross[:, :, width:]
    inverse(seqs)
    give_back(seqs)

    @pl.loop(0, seqs)
    def _(b):
        each_peer(lambda other: from_back(b, other).wait_recv())
        dx_ref[b] = back_recv[b].reshape(n * rows, width).T

    each_peer(lambda other: from_back(seqs, other).wait_recv())
    df_ref[...] = back_recv[seqs].reshape(n * rows, width).T

    @pl.loop(0, seqs + 1)
    def _(b):
        each_peer(lambda other: to_back(b, other).wait_send())


def write_out(dx_ref, df_ref, dx_hbm, df_hbm, sems):
    copies = [
        pltpu.make_async_copy(dx_ref, dx_hbm, sems.at[0]),
        pltpu.make_async_copy(df_ref, df_hbm, sems.at[1]),
    ]
    for copy in copies:
        copy.start()
    for copy in copies:
        copy.wait()


def tables(n, width):
    period = n * width
    turns = np.outer(np.arange(width), np.arange(width)) % width
    angle = turns * (2.0 * math.pi / width)
    cos, sin = np.cos(angle), np.sin(angle)
    table = np.block([[cos, -sin], [sin, cos]]).astype(np.float32)
    high = table.astype(ml_dtypes.bfloat16)
    low = (table - high.astype(np.float32)).astype(ml_dtypes.bfloat16)
    angle = np.outer(np.arange(n // 2 + 1), np.arange(width)) * (2.0 * math.pi / period)
    return high, low, np.cos(angle).astype(np.float32), np.sin(angle).astype(np.float32)


def body(n, nch, inputs, cotangent, filters):
    seqs, width, channels = inputs.shape
    rows = channels // n
    half = n // 2
    period = n * width
    factor = 1.0 / (period * math.sqrt(2.0 * period))
    high, low, cos, sin = (jnp.asarray(value) for value in tables(n, width))
    vmem = pl.BlockSpec(memory_space=pltpu.VMEM)
    anywhere = pl.BlockSpec(memory_space=pl.ANY)
    real = jnp.float32
    dma = pltpu.SemaphoreType.DMA
    grads = pl.pallas_call(
        functools.partial(kernel, n, nch, seqs, factor),
        out_shape=(
            pltpu.VMEM(inputs.shape, real),
            pltpu.VMEM(filters.shape, real),
        ),
        in_specs=[anywhere] * 7,
        out_specs=(vmem, vmem),
        scratch_shapes=[
            pltpu.VMEM(inputs.shape, real),
            pltpu.VMEM(inputs.shape, real),
            pltpu.VMEM(filters.shape, real),
            pltpu.VMEM(high.shape, high.dtype),
            pltpu.VMEM(low.shape, low.dtype),
            pltpu.VMEM(cos.shape, real),
            pltpu.VMEM(sin.shape, real),
            pltpu.VMEM((n, rows, width), real),
            pltpu.VMEM((seqs, n, 2, rows, width), real),
            pltpu.VMEM((n, rows, width), real),
            pltpu.VMEM((seqs, n, 2, rows, width), real),
            pltpu.VMEM((seqs + 1, n, rows, width), real),
            pltpu.VMEM((seqs + 1, n, rows, width), real),
            pltpu.VMEM((half + 1, 2 * rows, 2 * width), real),
            pltpu.VMEM((half + 1, 2 * rows, 2 * width), real),
            pltpu.VMEM((half + 1, rows, 2 * width), real),
            pltpu.VMEM((half + 1, rows, 2 * width), real),
            pltpu.VMEM((2, half + 1, rows, 2 * width), real),
            pltpu.VMEM((half + 1, rows, 2 * width), real),
            dma((seqs + 1, n)), dma((seqs + 1, n)),
            dma((seqs + 1, n)), dma((seqs + 1, n)),
            dma((2,)), dma((2,)), dma((seqs, 2)), dma((5,)),
        ],
        compiler_params=pltpu.CompilerParams(
            collective_id=0, has_side_effects=True, vmem_limit_bytes=56 * 2**20
        ),
    )(inputs, cotangent, filters, high, low, cos, sin)
    return tuple(pl.pallas_call(
        write_out,
        out_shape=(
            jax.ShapeDtypeStruct(inputs.shape, real),
            jax.ShapeDtypeStruct(filters.shape, real),
        ),
        in_specs=[vmem, vmem],
        out_specs=(anywhere, anywhere),
        scratch_shapes=[dma((2,))],
    )(*grads))


def solution(mesh):
    in_specs = (P(None, "ctx", "ch"), P(None, "ctx", "ch"), P("ctx", "ch"))
    out_specs = (P(None, "ctx", "ch"), P("ctx", "ch"))
    run = functools.partial(body, mesh.shape["ctx"], mesh.shape["ch"])
    return jax.shard_map(run, mesh=mesh, in_specs=in_specs, out_specs=out_specs, check_vma=False)
```

```python
import functools
import math

import jax
import jax.numpy as jnp
import ml_dtypes
import numpy as np
from jax import lax
from jax.experimental import pallas as pl
from jax.experimental.pallas import tpu as pltpu
from jax.sharding import PartitionSpec as P

MESH = pl.DeviceIdType.MESH


def plus(left, right):
    if left is None:
        return right
    return left if right is None else left + right


def minus(left, right):
    if right is None:
        return left
    return -right if left is None else left - right


def turn(value, cos, sin):
    real, imag = value
    if imag is None:
        return (real * cos, real * sin)
    return (real * cos - imag * sin, real * sin + imag * cos)


def real_forward(items):
    n = len(items)
    if n == 1:
        return [(items[0], None)]
    even, odd = real_forward(items[0::2]), real_forward(items[1::2])
    out = [None] * (n // 2 + 1)
    out[0] = (even[0][0] + odd[0][0], None)
    out[n // 2] = (even[0][0] - odd[0][0], None)
    for k in range(1, n // 4 + 1):
        if 4 * k == n:
            out[k] = (even[k][0], -odd[k][0])
            continue
        angle = -2.0 * math.pi * k / n
        turned = turn(odd[k], math.cos(angle), math.sin(angle))
        out[k] = (plus(even[k][0], turned[0]), plus(even[k][1], turned[1]))
        out[n // 2 - k] = (minus(even[k][0], turned[0]), minus(turned[1], even[k][1]))
    return out


def real_inverse(items, n):
    if n == 1:
        return [items[0][0]]
    first, last = items[0][0], items[n // 2][0]
    if n == 2:
        return [first + last, first - last]
    even, odd = [(first + last, None)], [(first - last, None)]
    for k in range(1, n // 4 + 1):
        real, imag = items[k]
        if 4 * k == n:
            even.append((2.0 * real, None))
            odd.append((-2.0 * imag, None))
            continue
        far_real, far_imag = items[n // 2 - k]
        angle = 2.0 * math.pi * k / n
        even.append((real + far_real, imag - far_imag))
        odd.append(turn((real - far_real, imag + far_imag), math.cos(angle), math.sin(angle)))
    out = [None] * n
    out[0::2] = real_inverse(even, n // 2)
    out[1::2] = real_inverse(odd, n // 2)
    return out


def split(value):
    high = value.astype(jnp.bfloat16)
    return high, (value - high.astype(jnp.float32)).astype(jnp.bfloat16)


def product(value, table_hi, table_lo):
    high, low = split(value)
    dot = functools.partial(jnp.dot, preferred_element_type=jnp.float32)
    return dot(high, table_hi) + (dot(low, table_hi) + dot(high, table_lo))


def kernel(
    n, nch, seqs, factor,
    x_hbm, g_hbm, f_hbm, hi_hbm, lo_hbm, cos_hbm, sin_hbm,
    dx_ref, df_ref,
    x_ref, g_ref, f_ref, hi_ref, lo_ref, cos_ref, sin_ref,
    send_f, send_d, recv_f, recv_d, back_send, back_recv,
    lhs, spec, eff, cross, mirror, flipped,
    fwd_send, fwd_recv, ret_send, ret_recv, pair_send, pair_recv, load_sem, table_sem,
):
    me = lax.axis_index("ctx")
    ch = lax.axis_index("ch")
    partner = nch - 1 - ch
    upper = (2 * ch) // nch
    width = x_ref.shape[1]
    rows = x_ref.shape[2] // n
    half = n // 2

    def chunk(owner):
        return owner + upper * (n - 1 - 2 * owner)

    def peer(step):
        mask = lax.rem(step + half - 2, n - 1) + 1
        other = me
        for bit in range(n.bit_length() - 1):
            weight = 2**bit
            other = other + lax.rem(mask // weight, 2) * weight * (1 - 2 * lax.rem(me // weight, 2))
        return other

    def load(b, which, source, target):
        return pltpu.make_async_copy(source.at[b], target.at[b], load_sem.at[b, which])

    def table(which, source, target):
        return pltpu.make_async_copy(source, target, table_sem.at[which])

    def to_filter(other):
        return pltpu.make_async_remote_copy(
            src_ref=send_f.at[chunk(other)], dst_ref=recv_f.at[me],
            send_sem=fwd_send.at[seqs, other], recv_sem=fwd_recv.at[seqs, me],
            device_id={"ctx": other}, device_id_type=MESH,
        )

    def from_filter(other):
        return pltpu.make_async_remote_copy(
            src_ref=send_f.at[chunk(other)], dst_ref=recv_f.at[other],
            send_sem=fwd_send.at[seqs, other], recv_sem=fwd_recv.at[seqs, other],
            device_id={"ctx": other}, device_id_type=MESH,
        )

    def to_data(b, other):
        return pltpu.make_async_remote_copy(
            src_ref=send_d.at[b, chunk(other)], dst_ref=recv_d.at[b, me],
            send_sem=fwd_send.at[b, other], recv_sem=fwd_recv.at[b, me],
            device_id={"ctx": other}, device_id_type=MESH,
        )

    def from_data(b, other):
        return pltpu.make_async_remote_copy(
            src_ref=send_d.at[b, chunk(other)], dst_ref=recv_d.at[b, other],
            send_sem=fwd_send.at[b, other], recv_sem=fwd_recv.at[b, other],
            device_id={"ctx": other}, device_id_type=MESH,
        )

    def to_back(b, other):
        return pltpu.make_async_remote_copy(
            src_ref=back_send.at[b, other], dst_ref=back_recv.at[b, chunk(me)],
            send_sem=ret_send.at[b, other], recv_sem=ret_recv.at[b, me],
            device_id={"ctx": other}, device_id_type=MESH,
        )

    def from_back(b, other):
        return pltpu.make_async_remote_copy(
            src_ref=back_send.at[b, other], dst_ref=back_recv.at[b, chunk(other)],
            send_sem=ret_send.at[b, other], recv_sem=ret_recv.at[b, other],
            device_id={"ctx": other}, device_id_type=MESH,
        )

    def to_pair(which, source):
        return pltpu.make_async_remote_copy(
            src_ref=source, dst_ref=mirror.at[which],
            send_sem=pair_send.at[which], recv_sem=pair_recv.at[which],
            device_id={"ch": partner}, device_id_type=MESH,
        )

    def each_peer(act):
        @pl.loop(1, n)
        def _(step):
            act(peer(step))

    def forward(arrays, count):
        for p, (real, imag) in enumerate(real_forward(arrays)):
            if p > 0:
                cos, sin = cos_ref[p : p + 1, :], sin_ref[p : p + 1, :]
                real, imag = turn((real, imag), cos, -sin)
            lhs[p, :count, :width] = real
            lhs[p, :count, width:] = jnp.zeros_like(real) if imag is None else imag
        flat = lhs[:, :count, :].reshape((half + 1) * count, 2 * width)
        out = product(flat, hi_ref[...], lo_ref[...])
        spec[:, :count, :] = out.reshape(half + 1, count, 2 * width)

    def inverse(b):
        flat = lhs[:, :rows, :].reshape((half + 1) * rows, 2 * width)
        out = product(flat, hi_ref[...], lo_ref[...])
        out = out.reshape(half + 1, rows, 2 * width) * factor
        items = []
        for p in range(half + 1):
            value = (out[p, :, :width], -out[p, :, width:])
            if p > 0:
                cos, sin = cos_ref[p : p + 1, :], sin_ref[p : p + 1, :]
                value = turn(value, cos, sin)
            items.append(value)
        for i, block in enumerate(real_inverse(items, n)):
            back_send[b, i] = block
        back_recv[b, chunk(me)] = back_send[b, me]

    def give_back(b):
        each_peer(lambda other: to_back(b, other).start())

    def add_mirror(which, target):
        for r in range(rows):
            flipped[:, r : r + 1, :] = mirror[which, :, rows - 1 - r : rows - r, :]
        target[:, :, :width] += flipped[:, :, :width]
        target[:, :, width:] -= flipped[:, :, width:]

    filter_load = table(0, f_hbm, f_ref)
    filter_load.start()

    barrier = pltpu.get_barrier_semaphore()
    each_peer(
        lambda other: pl.semaphore_signal(
            barrier, inc=1, device_id={"ctx": other}, device_id_type=MESH
        )
    )
    pl.semaphore_signal(barrier, inc=1, device_id={"ch": partner}, device_id_type=MESH)

    @pl.loop(0, seqs)
    def _(b):
        load(b, 0, g_hbm, g_ref).start()
        load(b, 1, x_hbm, x_ref).start()

    table_loads = [
        table(1, hi_hbm, hi_ref), table(2, lo_hbm, lo_ref),
        table(3, cos_hbm, cos_ref), table(4, sin_hbm, sin_ref),
    ]
    for copy in table_loads:
        copy.start()

    filter_load.wait()
    send_f[...] = f_ref[...].T.reshape(n, rows, width)
    pl.semaphore_wait(barrier, n)

    each_peer(lambda other: to_filter(other).start())
    recv_f[me] = send_f[chunk(me)]

    @pl.loop(0, seqs)
    def _(b):
        load(b, 0, g_hbm, g_ref).wait()
        load(b, 1, x_hbm, x_ref).wait()
        send_d[b, :, 0] = g_ref[b].T.reshape(n, rows, width)
        send_d[b, :, 1] = x_ref[b].T.reshape(n, rows, width)
        each_peer(lambda other: to_data(b, other).start())
        recv_d[b, me] = send_d[b, chunk(me)]

    for copy in table_loads:
        copy.wait()
    each_peer(lambda other: from_filter(other).wait_recv())
    forward([recv_f[i] for i in range(n)], rows)
    eff[...] = spec[:, :rows, :]
    swap_f = to_pair(0, eff)
    swap_f.start()
    cross[...] = jnp.zeros_like(cross)
    swap_f.wait()
    add_mirror(0, eff)

    def gradient(b):
        each_peer(lambda other: from_data(b, other).wait_recv())
        forward([recv_d[b, i].reshape(2 * rows, width) for i in range(n)], 2 * rows)
        g_re, g_im = spec[:, :rows, :width], spec[:, :rows, width:]
        x_re, x_im = spec[:, rows:, :width], spec[:, rows:, width:]
        cross[:, :, :width] += g_re * x_re + g_im * x_im
        cross[:, :, width:] += g_im * x_re - g_re * x_im
        e_re, e_im = eff[:, :, :width], eff[:, :, width:]
        lhs[:, :rows, :width] = e_re * g_re + e_im * g_im
        lhs[:, :rows, width:] = e_im * g_re - e_re * g_im
        inverse(b)

    pl.loop(0, seqs - 1)(gradient)
    give_back(0)
    each_peer(lambda other: to_filter(other).wait_send())

    @pl.loop(0, seqs)
    def _(b):
        each_peer(lambda other: to_data(b, other).wait_send())

    pl.loop(1, seqs - 1)(give_back)
    gradient(seqs - 1)
    swap_c = to_pair(1, cross)
    swap_c.start()
    give_back(seqs - 1)
    swap_c.wait()
    add_mirror(1, cross)
    lhs[:, :rows, :width] = cross[:, :, :width]
    lhs[:, :rows, width:] = -cross[:, :, width:]
    inverse(seqs)
    give_back(seqs)

    @pl.loop(0, seqs)
    def _(b):
        each_peer(lambda other: from_back(b, other).wait_recv())
        dx_ref[b] = back_recv[b].reshape(n * rows, width).T

    each_peer(lambda other: from_back(seqs, other).wait_recv())
    df_ref[...] = back_recv[seqs].reshape(n * rows, width).T

    @pl.loop(0, seqs + 1)
    def _(b):
        each_peer(lambda other: to_back(b, other).wait_send())


def write_out(dx_ref, df_ref, dx_hbm, df_hbm, sems):
    copies = [
        pltpu.make_async_copy(dx_ref, dx_hbm, sems.at[0]),
        pltpu.make_async_copy(df_ref, df_hbm, sems.at[1]),
    ]
    for copy in copies:
        copy.start()
    for copy in copies:
        copy.wait()


def tables(n, width):
    period = n * width
    turns = np.outer(np.arange(width), np.arange(width)) % width
    angle = turns * (2.0 * math.pi / width)
    cos, sin = np.cos(angle), np.sin(angle)
    table = np.block([[cos, -sin], [sin, cos]]).astype(np.float32)
    high = table.astype(ml_dtypes.bfloat16)
    low = (table - high.astype(np.float32)).astype(ml_dtypes.bfloat16)
    angle = np.outer(np.arange(n // 2 + 1), np.arange(width)) * (2.0 * math.pi / period)
    return high, low, np.cos(angle).astype(np.float32), np.sin(angle).astype(np.float32)


def body(n, nch, inputs, cotangent, filters):
    seqs, width, channels = inputs.shape
    rows = channels // n
    half = n // 2
    period = n * width
    factor = 1.0 / (period * math.sqrt(2.0 * period))
    high, low, cos, sin = (jnp.asarray(value) for value in tables(n, width))
    vmem = pl.BlockSpec(memory_space=pltpu.VMEM)
    anywhere = pl.BlockSpec(memory_space=pl.ANY)
    real = jnp.float32
    dma = pltpu.SemaphoreType.DMA
    grads = pl.pallas_call(
        functools.partial(kernel, n, nch, seqs, factor),
        out_shape=(
            pltpu.VMEM(inputs.shape, real),
            pltpu.VMEM(filters.shape, real),
        ),
        in_specs=[anywhere] * 7,
        out_specs=(vmem, vmem),
        scratch_shapes=[
            pltpu.VMEM(inputs.shape, real),
            pltpu.VMEM(inputs.shape, real),
            pltpu.VMEM(filters.shape, real),
            pltpu.VMEM(high.shape, high.dtype),
            pltpu.VMEM(low.shape, low.dtype),
            pltpu.VMEM(cos.shape, real),
            pltpu.VMEM(sin.shape, real),
            pltpu.VMEM((n, rows, width), real),
            pltpu.VMEM((seqs, n, 2, rows, width), real),
            pltpu.VMEM((n, rows, width), real),
            pltpu.VMEM((seqs, n, 2, rows, width), real),
            pltpu.VMEM((seqs + 1, n, rows, width), real),
            pltpu.VMEM((seqs + 1, n, rows, width), real),
            pltpu.VMEM((half + 1, 2 * rows, 2 * width), real),
            pltpu.VMEM((half + 1, 2 * rows, 2 * width), real),
            pltpu.VMEM((half + 1, rows, 2 * width), real),
            pltpu.VMEM((half + 1, rows, 2 * width), real),
            pltpu.VMEM((2, half + 1, rows, 2 * width), real),
            pltpu.VMEM((half + 1, rows, 2 * width), real),
            dma((seqs + 1, n)), dma((seqs + 1, n)),
            dma((seqs + 1, n)), dma((seqs + 1, n)),
            dma((2,)), dma((2,)), dma((seqs, 2)), dma((5,)),
        ],
        compiler_params=pltpu.CompilerParams(
            collective_id=0, has_side_effects=True, vmem_limit_bytes=56 * 2**20
        ),
    )(inputs, cotangent, filters, high, low, cos, sin)
    return tuple(pl.pallas_call(
        write_out,
        out_shape=(
            jax.ShapeDtypeStruct(inputs.shape, real),
            jax.ShapeDtypeStruct(filters.shape, real),
        ),
        in_specs=[vmem, vmem],
        out_specs=(anywhere, anywhere),
        scratch_shapes=[dma((2,))],
        compiler_params=pltpu.CompilerParams(vmem_limit_bytes=2**20),
    )(*grads))


def solution(mesh):
    in_specs = (P(None, "ctx", "ch"), P(None, "ctx", "ch"), P("ctx", "ch"))
    out_specs = (P(None, "ctx", "ch"), P("ctx", "ch"))
    run = functools.partial(body, mesh.shape["ctx"], mesh.shape["ch"])
    return jax.shard_map(run, mesh=mesh, in_specs=in_specs, out_specs=out_specs, check_vma=False)
```

```python
import functools
import math

import jax
import jax.numpy as jnp
import ml_dtypes
import numpy as np
from jax import lax
from jax.experimental import pallas as pl
from jax.experimental.pallas import tpu as pltpu
from jax.sharding import PartitionSpec as P

MESH = pl.DeviceIdType.MESH


def plus(left, right):
    if left is None:
        return right
    return left if right is None else left + right


def minus(left, right):
    if right is None:
        return left
    return -right if left is None else left - right


def turn(value, cos, sin):
    real, imag = value
    if imag is None:
        return (real * cos, real * sin)
    return (real * cos - imag * sin, real * sin + imag * cos)


def real_forward(items):
    n = len(items)
    if n == 1:
        return [(items[0], None)]
    even, odd = real_forward(items[0::2]), real_forward(items[1::2])
    out = [None] * (n // 2 + 1)
    out[0] = (even[0][0] + odd[0][0], None)
    out[n // 2] = (even[0][0] - odd[0][0], None)
    for k in range(1, n // 4 + 1):
        if 4 * k == n:
            out[k] = (even[k][0], -odd[k][0])
            continue
        angle = -2.0 * math.pi * k / n
        turned = turn(odd[k], math.cos(angle), math.sin(angle))
        out[k] = (plus(even[k][0], turned[0]), plus(even[k][1], turned[1]))
        out[n // 2 - k] = (minus(even[k][0], turned[0]), minus(turned[1], even[k][1]))
    return out


def real_inverse(items, n):
    if n == 1:
        return [items[0][0]]
    first, last = items[0][0], items[n // 2][0]
    if n == 2:
        return [first + last, first - last]
    even, odd = [(first + last, None)], [(first - last, None)]
    for k in range(1, n // 4 + 1):
        real, imag = items[k]
        if 4 * k == n:
            even.append((2.0 * real, None))
            odd.append((-2.0 * imag, None))
            continue
        far_real, far_imag = items[n // 2 - k]
        angle = 2.0 * math.pi * k / n
        even.append((real + far_real, imag - far_imag))
        odd.append(turn((real - far_real, imag + far_imag), math.cos(angle), math.sin(angle)))
    out = [None] * n
    out[0::2] = real_inverse(even, n // 2)
    out[1::2] = real_inverse(odd, n // 2)
    return out


def split(value):
    high = value.astype(jnp.bfloat16)
    return high, (value - high.astype(jnp.float32)).astype(jnp.bfloat16)


def product(value, table_hi, table_lo):
    high, low = split(value)
    dot = functools.partial(jnp.dot, preferred_element_type=jnp.float32)
    return dot(high, table_hi) + (dot(low, table_hi) + dot(high, table_lo))


def kernel(
    n, nch, seqs, factor,
    x_hbm, g_hbm, f_hbm, hi_hbm, lo_hbm, cos_hbm, sin_hbm,
    dx_ref, df_ref,
    x_ref, g_ref, f_ref, hi_ref, lo_ref, cos_ref, sin_ref,
    send_f, send_d, recv_f, recv_d, back_send, back_recv,
    lhs, spec, eff, cross, mirror, flipped,
    fwd_send, fwd_recv, ret_send, ret_recv, pair_send, pair_recv, load_sem, table_sem,
):
    me = lax.axis_index("ctx")
    ch = lax.axis_index("ch")
    partner = nch - 1 - ch
    upper = (2 * ch) // nch
    width = x_ref.shape[1]
    rows = x_ref.shape[2] // n
    half = n // 2

    def chunk(owner):
        return owner + upper * (n - 1 - 2 * owner)

    def peer(step):
        mask = step // 2 + lax.rem(step, 2) * half
        other = me
        for bit in range(n.bit_length() - 1):
            weight = 2**bit
            other = other + lax.rem(mask // weight, 2) * weight * (1 - 2 * lax.rem(me // weight, 2))
        return other

    def load(b, which, source, target):
        return pltpu.make_async_copy(source.at[b], target.at[b], load_sem.at[b, which])

    def table(which, source, target):
        return pltpu.make_async_copy(source, target, table_sem.at[which])

    def to_filter(other):
        return pltpu.make_async_remote_copy(
            src_ref=send_f.at[chunk(other)], dst_ref=recv_f.at[me],
            send_sem=fwd_send.at[seqs, other], recv_sem=fwd_recv.at[seqs, me],
            device_id={"ctx": other}, device_id_type=MESH,
        )

    def from_filter(other):
        return pltpu.make_async_remote_copy(
            src_ref=send_f.at[chunk(other)], dst_ref=recv_f.at[other],
            send_sem=fwd_send.at[seqs, other], recv_sem=fwd_recv.at[seqs, other],
            device_id={"ctx": other}, device_id_type=MESH,
        )

    def to_data(b, other):
        return pltpu.make_async_remote_copy(
            src_ref=send_d.at[b, chunk(other)], dst_ref=recv_d.at[b, me],
            send_sem=fwd_send.at[b, other], recv_sem=fwd_recv.at[b, me],
            device_id={"ctx": other}, device_id_type=MESH,
        )

    def from_data(b, other):
        return pltpu.make_async_remote_copy(
            src_ref=send_d.at[b, chunk(other)], dst_ref=recv_d.at[b, other],
            send_sem=fwd_send.at[b, other], recv_sem=fwd_recv.at[b, other],
            device_id={"ctx": other}, device_id_type=MESH,
        )

    def to_back(b, other):
        return pltpu.make_async_remote_copy(
            src_ref=back_send.at[b, other], dst_ref=back_recv.at[b, chunk(me)],
            send_sem=ret_send.at[b, other], recv_sem=ret_recv.at[b, me],
            device_id={"ctx": other}, device_id_type=MESH,
        )

    def from_back(b, other):
        return pltpu.make_async_remote_copy(
            src_ref=back_send.at[b, other], dst_ref=back_recv.at[b, chunk(other)],
            send_sem=ret_send.at[b, other], recv_sem=ret_recv.at[b, other],
            device_id={"ctx": other}, device_id_type=MESH,
        )

    def to_pair(which, source):
        return pltpu.make_async_remote_copy(
            src_ref=source, dst_ref=mirror.at[which],
            send_sem=pair_send.at[which], recv_sem=pair_recv.at[which],
            device_id={"ch": partner}, device_id_type=MESH,
        )

    def each_peer(act):
        @pl.loop(1, n)
        def _(step):
            act(peer(step))

    def forward(arrays, count):
        for p, (real, imag) in enumerate(real_forward(arrays)):
            if p > 0:
                cos, sin = cos_ref[p : p + 1, :], sin_ref[p : p + 1, :]
                real, imag = turn((real, imag), cos, -sin)
            lhs[p, :count, :width] = real
            lhs[p, :count, width:] = jnp.zeros_like(real) if imag is None else imag
        flat = lhs[:, :count, :].reshape((half + 1) * count, 2 * width)
        out = product(flat, hi_ref[...], lo_ref[...])
        spec[:, :count, :] = out.reshape(half + 1, count, 2 * width)

    def inverse(b):
        flat = lhs[:, :rows, :].reshape((half + 1) * rows, 2 * width)
        out = product(flat, hi_ref[...], lo_ref[...])
        out = out.reshape(half + 1, rows, 2 * width) * factor
        items = []
        for p in range(half + 1):
            value = (out[p, :, :width], -out[p, :, width:])
            if p > 0:
                cos, sin = cos_ref[p : p + 1, :], sin_ref[p : p + 1, :]
                value = turn(value, cos, sin)
            items.append(value)
        for i, block in enumerate(real_inverse(items, n)):
            back_send[b, i] = block
        back_recv[b, chunk(me)] = back_send[b, me]

    def give_back(b):
        each_peer(lambda other: to_back(b, other).start())

    def add_mirror(which, target):
        for r in range(rows):
            flipped[:, r : r + 1, :] = mirror[which, :, rows - 1 - r : rows - r, :]
        target[:, :, :width] += flipped[:, :, :width]
        target[:, :, width:] -= flipped[:, :, width:]

    filter_load = table(0, f_hbm, f_ref)
    filter_load.start()

    barrier = pltpu.get_barrier_semaphore()
    each_peer(
        lambda other: pl.semaphore_signal(
            barrier, inc=1, device_id={"ctx": other}, device_id_type=MESH
        )
    )
    pl.semaphore_signal(barrier, inc=1, device_id={"ch": partner}, device_id_type=MESH)

    @pl.loop(0, seqs)
    def _(b):
        load(b, 0, g_hbm, g_ref).start()
        load(b, 1, x_hbm, x_ref).start()

    table_loads = [
        table(1, hi_hbm, hi_ref), table(2, lo_hbm, lo_ref),
        table(3, cos_hbm, cos_ref), table(4, sin_hbm, sin_ref),
    ]
    for copy in table_loads:
        copy.start()

    filter_load.wait()
    send_f[...] = f_ref[...].T.reshape(n, rows, width)
    pl.semaphore_wait(barrier, n)

    each_peer(lambda other: to_filter(other).start())
    recv_f[me] = send_f[chunk(me)]

    @pl.loop(0, seqs)
    def _(b):
        load(b, 0, g_hbm, g_ref).wait()
        load(b, 1, x_hbm, x_ref).wait()
        send_d[b, :, 0] = g_ref[b].T.reshape(n, rows, width)
        send_d[b, :, 1] = x_ref[b].T.reshape(n, rows, width)
        each_peer(lambda other: to_data(b, other).start())
        recv_d[b, me] = send_d[b, chunk(me)]

    for copy in table_loads:
        copy.wait()
    each_peer(lambda other: from_filter(other).wait_recv())
    forward([recv_f[i] for i in range(n)], rows)
    eff[...] = spec[:, :rows, :]
    swap_f = to_pair(0, eff)
    swap_f.start()
    cross[...] = jnp.zeros_like(cross)
    swap_f.wait()
    add_mirror(0, eff)

    def gradient(b):
        each_peer(lambda other: from_data(b, other).wait_recv())
        forward([recv_d[b, i].reshape(2 * rows, width) for i in range(n)], 2 * rows)
        g_re, g_im = spec[:, :rows, :width], spec[:, :rows, width:]
        x_re, x_im = spec[:, rows:, :width], spec[:, rows:, width:]
        cross[:, :, :width] += g_re * x_re + g_im * x_im
        cross[:, :, width:] += g_im * x_re - g_re * x_im
        e_re, e_im = eff[:, :, :width], eff[:, :, width:]
        lhs[:, :rows, :width] = e_re * g_re + e_im * g_im
        lhs[:, :rows, width:] = e_im * g_re - e_re * g_im
        inverse(b)

    pl.loop(0, seqs - 1)(gradient)
    give_back(0)
    each_peer(lambda other: to_filter(other).wait_send())

    @pl.loop(0, seqs)
    def _(b):
        each_peer(lambda other: to_data(b, other).wait_send())

    pl.loop(1, seqs - 1)(give_back)
    gradient(seqs - 1)
    swap_c = to_pair(1, cross)
    swap_c.start()
    give_back(seqs - 1)
    swap_c.wait()
    add_mirror(1, cross)
    lhs[:, :rows, :width] = cross[:, :, :width]
    lhs[:, :rows, width:] = -cross[:, :, width:]
    inverse(seqs)
    give_back(seqs)

    @pl.loop(0, seqs)
    def _(b):
        each_peer(lambda other: from_back(b, other).wait_recv())
        dx_ref[b] = back_recv[b].reshape(n * rows, width).T

    each_peer(lambda other: from_back(seqs, other).wait_recv())
    df_ref[...] = back_recv[seqs].reshape(n * rows, width).T

    @pl.loop(0, seqs + 1)
    def _(b):
        each_peer(lambda other: to_back(b, other).wait_send())


def write_out(dx_ref, df_ref, dx_hbm, df_hbm, sems):
    copies = [
        pltpu.make_async_copy(dx_ref, dx_hbm, sems.at[0]),
        pltpu.make_async_copy(df_ref, df_hbm, sems.at[1]),
    ]
    for copy in copies:
        copy.start()
    for copy in copies:
        copy.wait()


def tables(n, width):
    period = n * width
    turns = np.outer(np.arange(width), np.arange(width)) % width
    angle = turns * (2.0 * math.pi / width)
    cos, sin = np.cos(angle), np.sin(angle)
    table = np.block([[cos, -sin], [sin, cos]]).astype(np.float32)
    high = table.astype(ml_dtypes.bfloat16)
    low = (table - high.astype(np.float32)).astype(ml_dtypes.bfloat16)
    angle = np.outer(np.arange(n // 2 + 1), np.arange(width)) * (2.0 * math.pi / period)
    return high, low, np.cos(angle).astype(np.float32), np.sin(angle).astype(np.float32)


def body(n, nch, inputs, cotangent, filters):
    seqs, width, channels = inputs.shape
    rows = channels // n
    half = n // 2
    period = n * width
    factor = 1.0 / (period * math.sqrt(2.0 * period))
    high, low, cos, sin = (jnp.asarray(value) for value in tables(n, width))
    vmem = pl.BlockSpec(memory_space=pltpu.VMEM)
    anywhere = pl.BlockSpec(memory_space=pl.ANY)
    real = jnp.float32
    dma = pltpu.SemaphoreType.DMA
    grads = pl.pallas_call(
        functools.partial(kernel, n, nch, seqs, factor),
        out_shape=(
            pltpu.VMEM(inputs.shape, real),
            pltpu.VMEM(filters.shape, real),
        ),
        in_specs=[anywhere] * 7,
        out_specs=(vmem, vmem),
        scratch_shapes=[
            pltpu.VMEM(inputs.shape, real),
            pltpu.VMEM(inputs.shape, real),
            pltpu.VMEM(filters.shape, real),
            pltpu.VMEM(high.shape, high.dtype),
            pltpu.VMEM(low.shape, low.dtype),
            pltpu.VMEM(cos.shape, real),
            pltpu.VMEM(sin.shape, real),
            pltpu.VMEM((n, rows, width), real),
            pltpu.VMEM((seqs, n, 2, rows, width), real),
            pltpu.VMEM((n, rows, width), real),
            pltpu.VMEM((seqs, n, 2, rows, width), real),
            pltpu.VMEM((seqs + 1, n, rows, width), real),
            pltpu.VMEM((seqs + 1, n, rows, width), real),
            pltpu.VMEM((half + 1, 2 * rows, 2 * width), real),
            pltpu.VMEM((half + 1, 2 * rows, 2 * width), real),
            pltpu.VMEM((half + 1, rows, 2 * width), real),
            pltpu.VMEM((half + 1, rows, 2 * width), real),
            pltpu.VMEM((2, half + 1, rows, 2 * width), real),
            pltpu.VMEM((half + 1, rows, 2 * width), real),
            dma((seqs + 1, n)), dma((seqs + 1, n)),
            dma((seqs + 1, n)), dma((seqs + 1, n)),
            dma((2,)), dma((2,)), dma((seqs, 2)), dma((5,)),
        ],
        compiler_params=pltpu.CompilerParams(
            collective_id=0, has_side_effects=True, vmem_limit_bytes=56 * 2**20
        ),
    )(inputs, cotangent, filters, high, low, cos, sin)
    return tuple(pl.pallas_call(
        write_out,
        out_shape=(
            jax.ShapeDtypeStruct(inputs.shape, real),
            jax.ShapeDtypeStruct(filters.shape, real),
        ),
        in_specs=[vmem, vmem],
        out_specs=(anywhere, anywhere),
        scratch_shapes=[dma((2,))],
        compiler_params=pltpu.CompilerParams(vmem_limit_bytes=2**20),
    )(*grads))


def solution(mesh):
    in_specs = (P(None, "ctx", "ch"), P(None, "ctx", "ch"), P("ctx", "ch"))
    out_specs = (P(None, "ctx", "ch"), P("ctx", "ch"))
    run = functools.partial(body, mesh.shape["ctx"], mesh.shape["ch"])
    return jax.shard_map(run, mesh=mesh, in_specs=in_specs, out_specs=out_specs, check_vma=False)
```

```python
import functools
import math

import jax
import jax.numpy as jnp
import ml_dtypes
import numpy as np
from jax import lax
from jax.experimental import pallas as pl
from jax.experimental.pallas import tpu as pltpu
from jax.sharding import PartitionSpec as P

MESH = pl.DeviceIdType.MESH


def plus(left, right):
    if left is None:
        return right
    return left if right is None else left + right


def minus(left, right):
    if right is None:
        return left
    return -right if left is None else left - right


def turn(value, cos, sin):
    real, imag = value
    if imag is None:
        return (real * cos, real * sin)
    return (real * cos - imag * sin, real * sin + imag * cos)


def real_forward(items):
    n = len(items)
    if n == 1:
        return [(items[0], None)]
    even, odd = real_forward(items[0::2]), real_forward(items[1::2])
    out = [None] * (n // 2 + 1)
    out[0] = (even[0][0] + odd[0][0], None)
    out[n // 2] = (even[0][0] - odd[0][0], None)
    for k in range(1, n // 4 + 1):
        if 4 * k == n:
            out[k] = (even[k][0], -odd[k][0])
            continue
        angle = -2.0 * math.pi * k / n
        turned = turn(odd[k], math.cos(angle), math.sin(angle))
        out[k] = (plus(even[k][0], turned[0]), plus(even[k][1], turned[1]))
        out[n // 2 - k] = (minus(even[k][0], turned[0]), minus(turned[1], even[k][1]))
    return out


def real_inverse(items, n):
    if n == 1:
        return [items[0][0]]
    first, last = items[0][0], items[n // 2][0]
    if n == 2:
        return [first + last, first - last]
    even, odd = [(first + last, None)], [(first - last, None)]
    for k in range(1, n // 4 + 1):
        real, imag = items[k]
        if 4 * k == n:
            even.append((2.0 * real, None))
            odd.append((-2.0 * imag, None))
            continue
        far_real, far_imag = items[n // 2 - k]
        angle = 2.0 * math.pi * k / n
        even.append((real + far_real, imag - far_imag))
        odd.append(turn((real - far_real, imag + far_imag), math.cos(angle), math.sin(angle)))
    out = [None] * n
    out[0::2] = real_inverse(even, n // 2)
    out[1::2] = real_inverse(odd, n // 2)
    return out


def split(value):
    high = value.astype(jnp.bfloat16)
    return high, (value - high.astype(jnp.float32)).astype(jnp.bfloat16)


def product(value, table_hi, table_lo):
    high, low = split(value)
    dot = functools.partial(jnp.dot, preferred_element_type=jnp.float32)
    return dot(high, table_hi) + (dot(low, table_hi) + dot(high, table_lo))


def kernel(
    n, nch, seqs, factor,
    x_hbm, g_hbm, f_hbm, hi_hbm, lo_hbm, cos_hbm, sin_hbm,
    dx_ref, df_ref,
    x_ref, g_ref, f_ref, hi_ref, lo_ref, cos_ref, sin_ref,
    send_f, send_d, recv_f, recv_d, back_send, back_recv,
    lhs, spec, eff, cross, mirror, flipped,
    fwd_send, fwd_recv, ret_send, ret_recv, pair_send, pair_recv, load_sem, table_sem,
):
    me = lax.axis_index("ctx")
    ch = lax.axis_index("ch")
    partner = nch - 1 - ch
    upper = (2 * ch) // nch
    width = x_ref.shape[1]
    rows = x_ref.shape[2] // n
    half = n // 2

    def chunk(owner):
        return owner + upper * (n - 1 - 2 * owner)

    def peer(step):
        mask = step // 2 + lax.rem(step, 2) * half
        other = me
        for bit in range(n.bit_length() - 1):
            weight = 2**bit
            other = other + lax.rem(mask // weight, 2) * weight * (1 - 2 * lax.rem(me // weight, 2))
        return other

    def load(b, which, source, target):
        return pltpu.make_async_copy(source.at[b], target.at[b], load_sem.at[b, which])

    def table(which, source, target):
        return pltpu.make_async_copy(source, target, table_sem.at[which])

    def to_filter(other):
        return pltpu.make_async_remote_copy(
            src_ref=send_f.at[chunk(other)], dst_ref=recv_f.at[me],
            send_sem=fwd_send.at[seqs, other], recv_sem=fwd_recv.at[seqs, me],
            device_id={"ctx": other}, device_id_type=MESH,
        )

    def from_filter(other):
        return pltpu.make_async_remote_copy(
            src_ref=send_f.at[chunk(other)], dst_ref=recv_f.at[other],
            send_sem=fwd_send.at[seqs, other], recv_sem=fwd_recv.at[seqs, other],
            device_id={"ctx": other}, device_id_type=MESH,
        )

    def to_data(b, other):
        return pltpu.make_async_remote_copy(
            src_ref=send_d.at[b, chunk(other)], dst_ref=recv_d.at[b, me],
            send_sem=fwd_send.at[b, other], recv_sem=fwd_recv.at[b, me],
            device_id={"ctx": other}, device_id_type=MESH,
        )

    def from_data(b, other):
        return pltpu.make_async_remote_copy(
            src_ref=send_d.at[b, chunk(other)], dst_ref=recv_d.at[b, other],
            send_sem=fwd_send.at[b, other], recv_sem=fwd_recv.at[b, other],
            device_id={"ctx": other}, device_id_type=MESH,
        )

    def to_back(b, other):
        return pltpu.make_async_remote_copy(
            src_ref=back_send.at[b, other], dst_ref=back_recv.at[b, chunk(me)],
            send_sem=ret_send.at[b, other], recv_sem=ret_recv.at[b, me],
            device_id={"ctx": other}, device_id_type=MESH,
        )

    def from_back(b, other):
        return pltpu.make_async_remote_copy(
            src_ref=back_send.at[b, other], dst_ref=back_recv.at[b, chunk(other)],
            send_sem=ret_send.at[b, other], recv_sem=ret_recv.at[b, other],
            device_id={"ctx": other}, device_id_type=MESH,
        )

    def to_pair(which, source):
        return pltpu.make_async_remote_copy(
            src_ref=source, dst_ref=mirror.at[which],
            send_sem=pair_send.at[which], recv_sem=pair_recv.at[which],
            device_id={"ch": partner}, device_id_type=MESH,
        )

    def each_peer(act):
        @pl.loop(1, n)
        def _(step):
            act(peer(step))

    def forward(arrays, count):
        for p, (real, imag) in enumerate(real_forward(arrays)):
            if p > 0:
                cos, sin = cos_ref[p : p + 1, :], sin_ref[p : p + 1, :]
                real, imag = turn((real, imag), cos, -sin)
            lhs[p, :count, :width] = real
            lhs[p, :count, width:] = jnp.zeros_like(real) if imag is None else imag
        flat = lhs[:, :count, :].reshape((half + 1) * count, 2 * width)
        out = product(flat, hi_ref[...], lo_ref[...])
        spec[:, :count, :] = out.reshape(half + 1, count, 2 * width)

    def inverse(b):
        flat = lhs[:, :rows, :].reshape((half + 1) * rows, 2 * width)
        out = product(flat, hi_ref[...], lo_ref[...])
        out = out.reshape(half + 1, rows, 2 * width) * factor
        items = []
        for p in range(half + 1):
            value = (out[p, :, :width], -out[p, :, width:])
            if p > 0:
                cos, sin = cos_ref[p : p + 1, :], sin_ref[p : p + 1, :]
                value = turn(value, cos, sin)
            items.append(value)
        for i, block in enumerate(real_inverse(items, n)):
            back_send[b, i] = block
        back_recv[b, chunk(me)] = back_send[b, me]

    def give_back(b):
        each_peer(lambda other: to_back(b, other).start())

    def add_mirror(which, target):
        for r in range(rows):
            flipped[:, r : r + 1, :] = mirror[which, :, rows - 1 - r : rows - r, :]
        target[:, :, :width] += flipped[:, :, :width]
        target[:, :, width:] -= flipped[:, :, width:]

    filter_load = table(0, f_hbm, f_ref)
    filter_load.start()

    barrier = pltpu.get_barrier_semaphore()
    each_peer(
        lambda other: pl.semaphore_signal(
            barrier, inc=1, device_id={"ctx": other}, device_id_type=MESH
        )
    )
    pl.semaphore_signal(barrier, inc=1, device_id={"ch": partner}, device_id_type=MESH)

    @pl.loop(0, seqs)
    def _(b):
        load(b, 0, g_hbm, g_ref).start()
        load(b, 1, x_hbm, x_ref).start()

    table_loads = [
        table(1, hi_hbm, hi_ref), table(2, lo_hbm, lo_ref),
        table(3, cos_hbm, cos_ref), table(4, sin_hbm, sin_ref),
    ]
    for copy in table_loads:
        copy.start()

    filter_load.wait()
    send_f[...] = f_ref[...].T.reshape(n, rows, width)
    pl.semaphore_wait(barrier, n)

    each_peer(lambda other: to_filter(other).start())
    recv_f[me] = send_f[chunk(me)]

    @pl.loop(0, seqs)
    def _(b):
        load(b, 0, g_hbm, g_ref).wait()
        load(b, 1, x_hbm, x_ref).wait()
        send_d[b, :, 0] = g_ref[b].T.reshape(n, rows, width)
        send_d[b, :, 1] = x_ref[b].T.reshape(n, rows, width)
        each_peer(lambda other: to_data(b, other).start())
        recv_d[b, me] = send_d[b, chunk(me)]

    for copy in table_loads:
        copy.wait()
    each_peer(lambda other: from_filter(other).wait_recv())
    forward([recv_f[i] for i in range(n)], rows)
    eff[...] = spec[:, :rows, :]
    swap_f = to_pair(0, eff)
    swap_f.start()
    cross[...] = jnp.zeros_like(cross)
    swap_f.wait()
    add_mirror(0, eff)

    def gradient(b):
        each_peer(lambda other: from_data(b, other).wait_recv())
        forward([recv_d[b, i].reshape(2 * rows, width) for i in range(n)], 2 * rows)
        g_re, g_im = spec[:, :rows, :width], spec[:, :rows, width:]
        x_re, x_im = spec[:, rows:, :width], spec[:, rows:, width:]
        cross[:, :, :width] += g_re * x_re + g_im * x_im
        cross[:, :, width:] += g_im * x_re - g_re * x_im
        e_re, e_im = eff[:, :, :width], eff[:, :, width:]
        lhs[:, :rows, :width] = e_re * g_re + e_im * g_im
        lhs[:, :rows, width:] = e_im * g_re - e_re * g_im
        inverse(b)

    @pl.loop(0, seqs - 1)
    def _(b):
        gradient(b)
        give_back(b)

    gradient(seqs - 1)
    swap_c = to_pair(1, cross)
    swap_c.start()
    give_back(seqs - 1)
    swap_c.wait()
    add_mirror(1, cross)
    lhs[:, :rows, :width] = cross[:, :, :width]
    lhs[:, :rows, width:] = -cross[:, :, width:]
    inverse(seqs)
    give_back(seqs)

    @pl.loop(0, seqs)
    def _(b):
        each_peer(lambda other: from_back(b, other).wait_recv())
        dx_ref[b] = back_recv[b].reshape(n * rows, width).T

    each_peer(lambda other: from_back(seqs, other).wait_recv())
    df_ref[...] = back_recv[seqs].reshape(n * rows, width).T

    each_peer(lambda other: to_filter(other).wait_send())

    @pl.loop(0, seqs)
    def _(b):
        each_peer(lambda other: to_data(b, other).wait_send())

    @pl.loop(0, seqs + 1)
    def _(b):
        each_peer(lambda other: to_back(b, other).wait_send())


def write_out(dx_ref, df_ref, dx_hbm, df_hbm, sems):
    copies = [
        pltpu.make_async_copy(dx_ref, dx_hbm, sems.at[0]),
        pltpu.make_async_copy(df_ref, df_hbm, sems.at[1]),
    ]
    for copy in copies:
        copy.start()
    for copy in copies:
        copy.wait()


def tables(n, width):
    period = n * width
    turns = np.outer(np.arange(width), np.arange(width)) % width
    angle = turns * (2.0 * math.pi / width)
    cos, sin = np.cos(angle), np.sin(angle)
    table = np.block([[cos, -sin], [sin, cos]]).astype(np.float32)
    high = table.astype(ml_dtypes.bfloat16)
    low = (table - high.astype(np.float32)).astype(ml_dtypes.bfloat16)
    angle = np.outer(np.arange(n // 2 + 1), np.arange(width)) * (2.0 * math.pi / period)
    return high, low, np.cos(angle).astype(np.float32), np.sin(angle).astype(np.float32)


def body(n, nch, inputs, cotangent, filters):
    seqs, width, channels = inputs.shape
    rows = channels // n
    half = n // 2
    period = n * width
    factor = 1.0 / (period * math.sqrt(2.0 * period))
    high, low, cos, sin = (jnp.asarray(value) for value in tables(n, width))
    vmem = pl.BlockSpec(memory_space=pltpu.VMEM)
    anywhere = pl.BlockSpec(memory_space=pl.ANY)
    real = jnp.float32
    dma = pltpu.SemaphoreType.DMA
    grads = pl.pallas_call(
        functools.partial(kernel, n, nch, seqs, factor),
        out_shape=(
            pltpu.VMEM(inputs.shape, real),
            pltpu.VMEM(filters.shape, real),
        ),
        in_specs=[anywhere] * 7,
        out_specs=(vmem, vmem),
        scratch_shapes=[
            pltpu.VMEM(inputs.shape, real),
            pltpu.VMEM(inputs.shape, real),
            pltpu.VMEM(filters.shape, real),
            pltpu.VMEM(high.shape, high.dtype),
            pltpu.VMEM(low.shape, low.dtype),
            pltpu.VMEM(cos.shape, real),
            pltpu.VMEM(sin.shape, real),
            pltpu.VMEM((n, rows, width), real),
            pltpu.VMEM((seqs, n, 2, rows, width), real),
            pltpu.VMEM((n, rows, width), real),
            pltpu.VMEM((seqs, n, 2, rows, width), real),
            pltpu.VMEM((seqs + 1, n, rows, width), real),
            pltpu.VMEM((seqs + 1, n, rows, width), real),
            pltpu.VMEM((half + 1, 2 * rows, 2 * width), real),
            pltpu.VMEM((half + 1, 2 * rows, 2 * width), real),
            pltpu.VMEM((half + 1, rows, 2 * width), real),
            pltpu.VMEM((half + 1, rows, 2 * width), real),
            pltpu.VMEM((2, half + 1, rows, 2 * width), real),
            pltpu.VMEM((half + 1, rows, 2 * width), real),
            dma((seqs + 1, n)), dma((seqs + 1, n)),
            dma((seqs + 1, n)), dma((seqs + 1, n)),
            dma((2,)), dma((2,)), dma((seqs, 2)), dma((5,)),
        ],
        compiler_params=pltpu.CompilerParams(
            collective_id=0, has_side_effects=True, vmem_limit_bytes=56 * 2**20
        ),
    )(inputs, cotangent, filters, high, low, cos, sin)
    return tuple(pl.pallas_call(
        write_out,
        out_shape=(
            jax.ShapeDtypeStruct(inputs.shape, real),
            jax.ShapeDtypeStruct(filters.shape, real),
        ),
        in_specs=[vmem, vmem],
        out_specs=(anywhere, anywhere),
        scratch_shapes=[dma((2,))],
        compiler_params=pltpu.CompilerParams(vmem_limit_bytes=2**20),
    )(*grads))


def solution(mesh):
    in_specs = (P(None, "ctx", "ch"), P(None, "ctx", "ch"), P("ctx", "ch"))
    out_specs = (P(None, "ctx", "ch"), P("ctx", "ch"))
    run = functools.partial(body, mesh.shape["ctx"], mesh.shape["ch"])
    return jax.shard_map(run, mesh=mesh, in_specs=in_specs, out_specs=out_specs, check_vma=False)
```

```python
import functools
import math

import jax
import jax.numpy as jnp
import ml_dtypes
import numpy as np
from jax import lax
from jax.experimental import pallas as pl
from jax.experimental.pallas import tpu as pltpu
from jax.sharding import PartitionSpec as P

MESH = pl.DeviceIdType.MESH


def plus(left, right):
    if left is None:
        return right
    return left if right is None else left + right


def minus(left, right):
    if right is None:
        return left
    return -right if left is None else left - right


def turn(value, cos, sin):
    real, imag = value
    if imag is None:
        return (real * cos, real * sin)
    return (real * cos - imag * sin, real * sin + imag * cos)


def real_forward(items):
    n = len(items)
    if n == 1:
        return [(items[0], None)]
    even, odd = real_forward(items[0::2]), real_forward(items[1::2])
    out = [None] * (n // 2 + 1)
    out[0] = (even[0][0] + odd[0][0], None)
    out[n // 2] = (even[0][0] - odd[0][0], None)
    for k in range(1, n // 4 + 1):
        if 4 * k == n:
            out[k] = (even[k][0], -odd[k][0])
            continue
        angle = -2.0 * math.pi * k / n
        turned = turn(odd[k], math.cos(angle), math.sin(angle))
        out[k] = (plus(even[k][0], turned[0]), plus(even[k][1], turned[1]))
        out[n // 2 - k] = (minus(even[k][0], turned[0]), minus(turned[1], even[k][1]))
    return out


def real_inverse(items, n):
    if n == 1:
        return [items[0][0]]
    first, last = items[0][0], items[n // 2][0]
    if n == 2:
        return [first + last, first - last]
    even, odd = [(first + last, None)], [(first - last, None)]
    for k in range(1, n // 4 + 1):
        real, imag = items[k]
        if 4 * k == n:
            even.append((2.0 * real, None))
            odd.append((-2.0 * imag, None))
            continue
        far_real, far_imag = items[n // 2 - k]
        angle = 2.0 * math.pi * k / n
        even.append((real + far_real, imag - far_imag))
        odd.append(turn((real - far_real, imag + far_imag), math.cos(angle), math.sin(angle)))
    out = [None] * n
    out[0::2] = real_inverse(even, n // 2)
    out[1::2] = real_inverse(odd, n // 2)
    return out


def split(value):
    high = value.astype(jnp.bfloat16)
    return high, (value - high.astype(jnp.float32)).astype(jnp.bfloat16)


def product(value, table_hi, table_lo):
    high, low = split(value)
    dot = functools.partial(jnp.dot, preferred_element_type=jnp.float32)
    return dot(high, table_hi) + (dot(low, table_hi) + dot(high, table_lo))


def kernel(
    n, nch, seqs, factor,
    x_hbm, g_hbm, f_hbm, hi_hbm, lo_hbm, cos_hbm, sin_hbm,
    dx_ref, df_ref,
    x_ref, g_ref, f_ref, hi_ref, lo_ref, cos_ref, sin_ref,
    send_f, send_d, recv_f, recv_d, back_send, back_recv,
    lhs, spec, eff, cross, mirror, flipped,
    fwd_send, fwd_recv, ret_send, ret_recv, pair_send, pair_recv, load_sem, table_sem,
):
    me = lax.axis_index("ctx")
    ch = lax.axis_index("ch")
    partner = nch - 1 - ch
    upper = (2 * ch) // nch
    width = x_ref.shape[1]
    rows = x_ref.shape[2] // n
    half = n // 2

    def chunk(owner):
        return owner + upper * (n - 1 - 2 * owner)

    def peer(step):
        mask = step // 2 + lax.rem(step, 2) * half
        other = me
        for bit in range(n.bit_length() - 1):
            weight = 2**bit
            other = other + lax.rem(mask // weight, 2) * weight * (1 - 2 * lax.rem(me // weight, 2))
        return other

    def load(b, which, source, target):
        return pltpu.make_async_copy(source.at[b], target.at[b], load_sem.at[b, which])

    def table(which, source, target):
        return pltpu.make_async_copy(source, target, table_sem.at[which])

    def to_filter(other):
        return pltpu.make_async_remote_copy(
            src_ref=send_f.at[chunk(other)], dst_ref=recv_f.at[me],
            send_sem=fwd_send.at[seqs, other], recv_sem=fwd_recv.at[seqs, me],
            device_id={"ctx": other}, device_id_type=MESH,
        )

    def from_filter(other):
        return pltpu.make_async_remote_copy(
            src_ref=send_f.at[chunk(other)], dst_ref=recv_f.at[other],
            send_sem=fwd_send.at[seqs, other], recv_sem=fwd_recv.at[seqs, other],
            device_id={"ctx": other}, device_id_type=MESH,
        )

    def to_data(b, other):
        return pltpu.make_async_remote_copy(
            src_ref=send_d.at[b, chunk(other)], dst_ref=recv_d.at[b, me],
            send_sem=fwd_send.at[b, other], recv_sem=fwd_recv.at[b, me],
            device_id={"ctx": other}, device_id_type=MESH,
        )

    def from_data(b, other):
        return pltpu.make_async_remote_copy(
            src_ref=send_d.at[b, chunk(other)], dst_ref=recv_d.at[b, other],
            send_sem=fwd_send.at[b, other], recv_sem=fwd_recv.at[b, other],
            device_id={"ctx": other}, device_id_type=MESH,
        )

    def to_back(b, other):
        return pltpu.make_async_remote_copy(
            src_ref=back_send.at[b, other], dst_ref=back_recv.at[b, chunk(me)],
            send_sem=ret_send.at[b, other], recv_sem=ret_recv.at[b, me],
            device_id={"ctx": other}, device_id_type=MESH,
        )

    def from_back(b, other):
        return pltpu.make_async_remote_copy(
            src_ref=back_send.at[b, other], dst_ref=back_recv.at[b, chunk(other)],
            send_sem=ret_send.at[b, other], recv_sem=ret_recv.at[b, other],
            device_id={"ctx": other}, device_id_type=MESH,
        )

    def to_pair(which, source):
        return pltpu.make_async_remote_copy(
            src_ref=source, dst_ref=mirror.at[which],
            send_sem=pair_send.at[which], recv_sem=pair_recv.at[which],
            device_id={"ch": partner}, device_id_type=MESH,
        )

    def each_peer(act):
        @pl.loop(1, n)
        def _(step):
            act(peer(step))

    def forward(arrays, count):
        for p, (real, imag) in enumerate(real_forward(arrays)):
            if p > 0:
                cos, sin = cos_ref[p : p + 1, :], sin_ref[p : p + 1, :]
                real, imag = turn((real, imag), cos, -sin)
            lhs[p, :count, :width] = real
            lhs[p, :count, width:] = jnp.zeros_like(real) if imag is None else imag
        flat = lhs[:, :count, :].reshape((half + 1) * count, 2 * width)
        out = product(flat, hi_ref[...], lo_ref[...])
        spec[:, :count, :] = out.reshape(half + 1, count, 2 * width)

    def inverse(b):
        flat = lhs[:, :rows, :].reshape((half + 1) * rows, 2 * width)
        out = product(flat, hi_ref[...], lo_ref[...])
        out = out.reshape(half + 1, rows, 2 * width) * factor
        items = []
        for p in range(half + 1):
            value = (out[p, :, :width], -out[p, :, width:])
            if p > 0:
                cos, sin = cos_ref[p : p + 1, :], sin_ref[p : p + 1, :]
                value = turn(value, cos, sin)
            items.append(value)
        for i, block in enumerate(real_inverse(items, n)):
            back_send[b, i] = block
        back_recv[b, chunk(me)] = back_send[b, me]

    def give_back(b):
        each_peer(lambda other: to_back(b, other).start())

    def add_mirror(which, target):
        for r in range(rows):
            flipped[:, r : r + 1, :] = mirror[which, :, rows - 1 - r : rows - r, :]
        target[:, :, :width] += flipped[:, :, :width]
        target[:, :, width:] -= flipped[:, :, width:]

    filter_load = table(0, f_hbm, f_ref)
    filter_load.start()

    barrier = pltpu.get_barrier_semaphore()
    each_peer(
        lambda other: pl.semaphore_signal(
            barrier, inc=1, device_id={"ctx": other}, device_id_type=MESH
        )
    )
    pl.semaphore_signal(barrier, inc=1, device_id={"ch": partner}, device_id_type=MESH)

    @pl.loop(0, seqs)
    def _(b):
        load(b, 0, g_hbm, g_ref).start()
        load(b, 1, x_hbm, x_ref).start()

    table_loads = [
        table(1, hi_hbm, hi_ref), table(2, lo_hbm, lo_ref),
        table(3, cos_hbm, cos_ref), table(4, sin_hbm, sin_ref),
    ]
    for copy in table_loads:
        copy.start()

    filter_load.wait()
    send_f[...] = f_ref[...].T.reshape(n, rows, width)
    pl.semaphore_wait(barrier, n)

    each_peer(lambda other: to_filter(other).start())
    recv_f[me] = send_f[chunk(me)]

    first = min(2, seqs)

    def prepare(b):
        load(b, 0, g_hbm, g_ref).wait()
        load(b, 1, x_hbm, x_ref).wait()
        send_d[b, :, 0] = g_ref[b].T.reshape(n, rows, width)
        send_d[b, :, 1] = x_ref[b].T.reshape(n, rows, width)
        each_peer(lambda other: to_data(b, other).start())
        recv_d[b, me] = send_d[b, chunk(me)]

    pl.loop(0, first)(prepare)

    for copy in table_loads:
        copy.wait()
    each_peer(lambda other: from_filter(other).wait_recv())
    forward([recv_f[i] for i in range(n)], rows)
    eff[...] = spec[:, :rows, :]
    swap_f = to_pair(0, eff)
    swap_f.start()
    cross[...] = jnp.zeros_like(cross)
    swap_f.wait()
    add_mirror(0, eff)

    def gradient(b):
        each_peer(lambda other: from_data(b, other).wait_recv())
        forward([recv_d[b, i].reshape(2 * rows, width) for i in range(n)], 2 * rows)
        g_re, g_im = spec[:, :rows, :width], spec[:, :rows, width:]
        x_re, x_im = spec[:, rows:, :width], spec[:, rows:, width:]
        cross[:, :, :width] += g_re * x_re + g_im * x_im
        cross[:, :, width:] += g_im * x_re - g_re * x_im
        e_re, e_im = eff[:, :, :width], eff[:, :, width:]
        lhs[:, :rows, :width] = e_re * g_re + e_im * g_im
        lhs[:, :rows, width:] = e_im * g_re - e_re * g_im
        inverse(b)

    @pl.loop(0, seqs - first)
    def _(b):
        each_peer(lambda other: to_data(b, other).wait_send())
        prepare(b + first)
        gradient(b)

    pl.loop(seqs - first, seqs - 1)(gradient)
    give_back(0)
    each_peer(lambda other: to_filter(other).wait_send())

    @pl.loop(seqs - first, seqs)
    def _(b):
        each_peer(lambda other: to_data(b, other).wait_send())

    pl.loop(1, seqs - 1)(give_back)
    gradient(seqs - 1)
    swap_c = to_pair(1, cross)
    swap_c.start()
    give_back(seqs - 1)
    swap_c.wait()
    add_mirror(1, cross)
    lhs[:, :rows, :width] = cross[:, :, :width]
    lhs[:, :rows, width:] = -cross[:, :, width:]
    inverse(seqs)
    give_back(seqs)

    @pl.loop(0, seqs)
    def _(b):
        each_peer(lambda other: from_back(b, other).wait_recv())
        dx_ref[b] = back_recv[b].reshape(n * rows, width).T

    each_peer(lambda other: from_back(seqs, other).wait_recv())
    df_ref[...] = back_recv[seqs].reshape(n * rows, width).T

    @pl.loop(0, seqs + 1)
    def _(b):
        each_peer(lambda other: to_back(b, other).wait_send())


def write_out(dx_ref, df_ref, dx_hbm, df_hbm, sems):
    copies = [
        pltpu.make_async_copy(dx_ref, dx_hbm, sems.at[0]),
        pltpu.make_async_copy(df_ref, df_hbm, sems.at[1]),
    ]
    for copy in copies:
        copy.start()
    for copy in copies:
        copy.wait()


def tables(n, width):
    period = n * width
    turns = np.outer(np.arange(width), np.arange(width)) % width
    angle = turns * (2.0 * math.pi / width)
    cos, sin = np.cos(angle), np.sin(angle)
    table = np.block([[cos, -sin], [sin, cos]]).astype(np.float32)
    high = table.astype(ml_dtypes.bfloat16)
    low = (table - high.astype(np.float32)).astype(ml_dtypes.bfloat16)
    angle = np.outer(np.arange(n // 2 + 1), np.arange(width)) * (2.0 * math.pi / period)
    return high, low, np.cos(angle).astype(np.float32), np.sin(angle).astype(np.float32)


def body(n, nch, inputs, cotangent, filters):
    seqs, width, channels = inputs.shape
    rows = channels // n
    half = n // 2
    period = n * width
    factor = 1.0 / (period * math.sqrt(2.0 * period))
    high, low, cos, sin = (jnp.asarray(value) for value in tables(n, width))
    vmem = pl.BlockSpec(memory_space=pltpu.VMEM)
    anywhere = pl.BlockSpec(memory_space=pl.ANY)
    real = jnp.float32
    dma = pltpu.SemaphoreType.DMA
    grads = pl.pallas_call(
        functools.partial(kernel, n, nch, seqs, factor),
        out_shape=(
            pltpu.VMEM(inputs.shape, real),
            pltpu.VMEM(filters.shape, real),
        ),
        in_specs=[anywhere] * 7,
        out_specs=(vmem, vmem),
        scratch_shapes=[
            pltpu.VMEM(inputs.shape, real),
            pltpu.VMEM(inputs.shape, real),
            pltpu.VMEM(filters.shape, real),
            pltpu.VMEM(high.shape, high.dtype),
            pltpu.VMEM(low.shape, low.dtype),
            pltpu.VMEM(cos.shape, real),
            pltpu.VMEM(sin.shape, real),
            pltpu.VMEM((n, rows, width), real),
            pltpu.VMEM((seqs, n, 2, rows, width), real),
            pltpu.VMEM((n, rows, width), real),
            pltpu.VMEM((seqs, n, 2, rows, width), real),
            pltpu.VMEM((seqs + 1, n, rows, width), real),
            pltpu.VMEM((seqs + 1, n, rows, width), real),
            pltpu.VMEM((half + 1, 2 * rows, 2 * width), real),
            pltpu.VMEM((half + 1, 2 * rows, 2 * width), real),
            pltpu.VMEM((half + 1, rows, 2 * width), real),
            pltpu.VMEM((half + 1, rows, 2 * width), real),
            pltpu.VMEM((2, half + 1, rows, 2 * width), real),
            pltpu.VMEM((half + 1, rows, 2 * width), real),
            dma((seqs + 1, n)), dma((seqs + 1, n)),
            dma((seqs + 1, n)), dma((seqs + 1, n)),
            dma((2,)), dma((2,)), dma((seqs, 2)), dma((5,)),
        ],
        compiler_params=pltpu.CompilerParams(
            collective_id=0, has_side_effects=True, vmem_limit_bytes=56 * 2**20
        ),
    )(inputs, cotangent, filters, high, low, cos, sin)
    return tuple(pl.pallas_call(
        write_out,
        out_shape=(
            jax.ShapeDtypeStruct(inputs.shape, real),
            jax.ShapeDtypeStruct(filters.shape, real),
        ),
        in_specs=[vmem, vmem],
        out_specs=(anywhere, anywhere),
        scratch_shapes=[dma((2,))],
        compiler_params=pltpu.CompilerParams(vmem_limit_bytes=2**20),
    )(*grads))


def solution(mesh):
    in_specs = (P(None, "ctx", "ch"), P(None, "ctx", "ch"), P("ctx", "ch"))
    out_specs = (P(None, "ctx", "ch"), P("ctx", "ch"))
    run = functools.partial(body, mesh.shape["ctx"], mesh.shape["ch"])
    return jax.shard_map(run, mesh=mesh, in_specs=in_specs, out_specs=out_specs, check_vma=False)
```
